32 devices in a mesh: gx: 4 (over y, x), gy: 8 (over z, core).
Axes of the slice: x: 2, y: 2, z: 4, core: 2. Of those that a mesh axis runs over, the one named last changes fastest.
Arguments:
- features: bfloat16 [4, 8, 32, 8, 8, 512], P('gx', 'gy'), may hold values from -6 to 6
- occupancy: int32 [4, 8, 32, 25], P('gx', 'gy'), may hold values from 0 to 2097151, as said below
- neighbors: int32 [4, 8, 32, 27], P('gx', 'gy'), may hold values from 0 to 48, as said below
- face_lists: int32 [4, 8, 8], P('gx', 'gy'), may hold values from 0 to 31, as said below
- face_relays: int32 [4, 8, 8], P('gx', 'gy'), may hold values from 0 to 39, as said below
- send_slots: int32 [4, 8, 8, 4], P('gx', 'gy'), may hold values from -1 to 31, as said below
- receive_order: int32 [4, 8, 16], P('gx', 'gy'), may hold values from 0 to 31, as said below
- weights: bfloat16 [27, 64, 64], replicated, may hold values from -0.15625 to 0.15625
- channel_bias: float32 [64], replicated, may hold values from -3 to 3
Outputs:
- conv_out: bfloat16 [4, 8, 16, 8, 8, 512], P('gx', 'gy')
The draws below stay inside these ranges and needn't reach their ends.
Inputs may be any that keep to these rules, and one draw needn't show every extreme that they name: `occupancy`: bit k of word w of a held block is voxel 21 * w + k; bits past voxel 8 * 8 * 8 - 1 are zero; slots that hold no block have all words zero. `neighbors`: entries name pool blocks: held slots below 32, then blocks received across faces, then the zero block 48; entry 13 is the block's own slot; other held entries name occupied slots, or any slot where the device holds none. `face_lists`: entries name slots of the device that hold blocks, or any slot where the device holds none. `face_relays`: entries below 32 name occupied held slots, or any slot where the device holds none; the others name blocks received from gy neighbours. `send_slots`: device d of a gx index sends the same number c_d of items, 0 or more, to every device of that gx index, in items q < c_d, and -1 in the others; every occupied held slot is sent exactly once; in every gx index some device has c_d = 4. `receive_order`: every device receives exactly 16 used items; its rows name each of them exactly once.
All inputs are finite; a program needn't handle non-finite values.
Results may differ from the reference program's by a relative error of at most 0.001.
Values may be sent and summed in bfloat16 or wider, within the bound.
No kernel may reach another device: no remote copies, remote signals or barrier semaphores. Data moves between devices by JAX's collectives and lax.ppermute only.
A program may use at most 128 MiB of HBM per device.

```python
import jax
import jax.numpy as jnp
import numpy as np
from jax import lax

C = 64
BS = 8
OUT_BLOCKS = 16
HOME_SLOTS = 32
PEER_SLOTS = 4
FACE = 4
WORDS = 25
POOL = 49
N_GX = 4
N_GY = 8


def block_plan(key):
    base_key = jax.random.fold_in(key, 7)
    heavy_key, token_key, order_key = jax.random.split(base_key, 3)
    heavy = jax.random.randint(heavy_key, (N_GX, 1), 0, N_GY)
    tokens = N_GY * PEER_SLOTS

    def permute_tokens(row_key):
        return jax.random.permutation(row_key, tokens).astype(jnp.int32)
    scores = jax.vmap(permute_tokens)(jax.random.split(token_key, N_GX))
    token_ids = jnp.arange(tokens, dtype=jnp.int32)
    owner = token_ids // PEER_SLOTS
    first_item = (token_ids % PEER_SLOTS == 0).astype(jnp.int32)
    adjusted = scores + tokens * (1 - first_item)[None, :]
    adjusted = jnp.where(owner[None, :] == heavy, adjusted + 2 * tokens, adjusted)
    ranks = jnp.argsort(jnp.argsort(adjusted, axis=1, stable=True), axis=1, stable=True)
    chosen = (ranks < OUT_BLOCKS - PEER_SLOTS).astype(jnp.int32)
    counts = chosen.reshape(N_GX, N_GY, PEER_SLOTS).sum(axis=2)
    counts = jnp.where(jnp.arange(N_GY, dtype=jnp.int32)[None, :] == heavy, PEER_SLOTS, counts).astype(jnp.int32)

    def permute_slots(row_key):
        return jax.random.permutation(row_key, HOME_SLOTS).astype(jnp.int32)
    values = jax.vmap(permute_slots)(jax.random.split(order_key, N_GX * N_GY)).reshape(N_GX, N_GY, HOME_SLOTS)
    inverse = jnp.argsort(values, axis=2, stable=True).astype(jnp.int32)
    return (counts, values, inverse)


def pick_live(key, inverse, counts, shape):
    upper_bound = jnp.maximum(N_GY * counts, 1)
    extra = (1,) * (len(shape) - 2)
    ranks = jax.random.randint(key, shape, 0, upper_bound.reshape(upper_bound.shape + extra))
    flat = jnp.take_along_axis(inverse, ranks.reshape(N_GX, N_GY, -1), axis=2)
    return flat.reshape(shape)


def draw_occupancy(key, part):
    counts, values, inverse = block_plan(key)
    live = values < (N_GY * counts)[..., None]
    words = jax.random.randint(jax.random.fold_in(key, 11), (N_GX, N_GY, HOME_SLOTS, WORDS), 0, 2 ** 21)
    top_bits = BS ** 3 - 21 * (WORDS - 1)
    word_limit = np.full(WORDS, 2 ** 21 - 1, dtype=np.int32)
    word_limit[-1] = 2 ** top_bits - 1
    return jnp.where(live[..., None], words & jnp.asarray(word_limit), 0).astype(jnp.int32)


def draw_neighbors(key, part):
    counts, values, inverse = block_plan(key)
    shape = (N_GX, N_GY, HOME_SLOTS, 27)
    kind = jax.random.randint(jax.random.fold_in(key, 21), shape, 0, 10)
    local = pick_live(jax.random.fold_in(key, 22), inverse, counts, shape)
    remote = HOME_SLOTS + jax.random.randint(jax.random.fold_in(key, 23), shape, 0, 4 * FACE)
    picked = jnp.where(kind < 3, local, jnp.where(kind < 9, remote, POOL - 1))
    own_slot = jnp.broadcast_to(jnp.arange(HOME_SLOTS, dtype=jnp.int32)[None, None, :, None], shape)
    center = jnp.arange(27, dtype=jnp.int32)[None, None, None, :] == 13
    return jnp.where(center, own_slot, picked).astype(jnp.int32)


def draw_face_lists(key, part):
    counts, values, inverse = block_plan(key)
    return pick_live(jax.random.fold_in(key, 31), inverse, counts, (N_GX, N_GY, 2 * FACE)).astype(jnp.int32)


def draw_face_relays(key, part):
    counts, values, inverse = block_plan(key)
    shape = (N_GX, N_GY, 2 * FACE)
    kind = jax.random.randint(jax.random.fold_in(key, 41), shape, 0, 2)
    local = pick_live(jax.random.fold_in(key, 42), inverse, counts, shape)
    remote = HOME_SLOTS + jax.random.randint(jax.random.fold_in(key, 43), shape, 0, 2 * FACE)
    return jnp.where(kind == 0, local, remote).astype(jnp.int32)


def draw_send_slots(key, part):
    counts, values, inverse = block_plan(key)
    target = jnp.arange(N_GY, dtype=jnp.int32)[None, None, :, None]
    item_index = jnp.arange(PEER_SLOTS, dtype=jnp.int32)[None, None, None, :]
    sent = counts[:, :, None, None]
    position = jnp.minimum(target * sent + item_index, HOME_SLOTS - 1)
    position = jnp.broadcast_to(position, (N_GX, N_GY, N_GY, PEER_SLOTS))
    held = jnp.take_along_axis(inverse, position.reshape(N_GX, N_GY, -1), axis=2).reshape(N_GX, N_GY, N_GY, PEER_SLOTS)
    return jnp.where(item_index < sent, held, -1).astype(jnp.int32)


def draw_receive_order(key, part):
    counts, values, inverse = block_plan(key)
    used = (jnp.arange(PEER_SLOTS, dtype=jnp.int32)[None, None, :] < counts[:, :, None]).reshape(N_GX, 1, N_GY * PEER_SLOTS)

    def permute_items(row_key):
        return jax.random.permutation(row_key, N_GY * PEER_SLOTS).astype(jnp.int32)
    scores = jax.vmap(permute_items)(jax.random.split(jax.random.fold_in(key, 51), N_GX * N_GY)).reshape(N_GX, N_GY, N_GY * PEER_SLOTS)
    adjusted = jnp.where(used, scores, scores + N_GY * PEER_SLOTS)
    return jnp.argsort(adjusted, axis=2, stable=True)[:, :, :OUT_BLOCKS].astype(jnp.int32)


def block_levels(rng, dims, cuts, least, top_value):
    def one(dim, parts):
        heights = jax.random.uniform(jax.random.fold_in(jax.random.fold_in(rng, 6), dim), (parts,), jnp.float32, least / len(cuts), top_value / len(cuts))
        return jnp.repeat(jnp.exp(heights), dims[dim] // parts).reshape((-1,) + (1,) * (len(dims) - dim - 1))

    level = one(*cuts[0])
    for cut in cuts[1:]:
        level = level * one(*cut)
    return level


def centred(rng, shape, width, bound, pieces=(), kind=jnp.bfloat16):
    values = width * jax.random.normal(rng, shape, jnp.float32)
    if pieces:
        values = values * block_levels(rng, shape, pieces, -0.22, 0.18)
    return jnp.clip(values, -bound, bound).astype(kind)


def setup_inputs(seed: int = 0) -> dict:
    streams_of = jax.random.split(jax.random.key(seed), 10)
    return {
        "features": centred(streams_of[0], (N_GX, N_GY, HOME_SLOTS, BS, BS, BS * C), 1.0, 6.0, ((0, 4), (1, 8))),
        "occupancy": draw_occupancy(jax.random.fold_in(streams_of[9], 71), 0),
        "neighbors": draw_neighbors(jax.random.fold_in(streams_of[9], 71), 0),
        "face_lists": draw_face_lists(jax.random.fold_in(streams_of[9], 71), 0),
        "face_relays": draw_face_relays(jax.random.fold_in(streams_of[9], 71), 0),
        "send_slots": draw_send_slots(jax.random.fold_in(streams_of[9], 71), 0),
        "receive_order": draw_receive_order(jax.random.fold_in(streams_of[9], 71), 0),
        "weights": centred(streams_of[7], (27, C, C), (27 * C) ** -0.5, 0.15625),
        "channel_bias": centred(streams_of[8], (C,), 0.5, 3.0, (), jnp.float32),
    }


def unpack_bits(mask_words):
    voxels = np.arange(BS ** 3)
    picked = jnp.take(mask_words, jnp.asarray(voxels // 21, dtype=jnp.int32), axis=-1)
    occupied = jnp.right_shift(picked, jnp.asarray(voxels % 21, dtype=jnp.int32)) & 1
    return occupied.reshape(mask_words.shape[:-1] + (BS, BS, BS))


def apply_mask(blocks, mask_words):
    occupied = unpack_bits(mask_words).astype(blocks.dtype)
    spread = blocks.reshape(blocks.shape[:-1] + (BS, C)) * occupied[..., None]
    return spread.reshape(blocks.shape)


def assemble(block_pool, neighbor_rows):
    bounds = ((BS - 1, BS), (0, BS), (0, 1))
    planes = []
    for depth_x in range(3):
        row_parts = []
        for depth_y in range(3):
            column_parts = []
            for depth_z in range(3):
                section = block_pool[:, bounds[depth_x][0]:bounds[depth_x][1], bounds[depth_y][0]:bounds[depth_y][1], bounds[depth_z][0] * C:bounds[depth_z][1] * C]
                column_parts.append(jnp.take(section, neighbor_rows[:, 9 * depth_x + 3 * depth_y + depth_z], axis=0))
            row_parts.append(jnp.concatenate(column_parts, axis=3))
        planes.append(jnp.concatenate(row_parts, axis=2))
    return jnp.concatenate(planes, axis=1)


def convolve(tiles, weights, channel_bias, occupied):
    block_count = tiles.shape[0]
    shaped = tiles.astype(jnp.float32).reshape(block_count, BS + 2, BS + 2, BS + 2, C)
    weights_wide = weights.astype(jnp.float32)
    summed = jnp.zeros((block_count, BS, BS, BS, C), jnp.float32)
    for depth_x in range(3):
        for depth_y in range(3):
            for depth_z in range(3):
                window = shaped[:, depth_x:depth_x + BS, depth_y:depth_y + BS, depth_z:depth_z + BS, :]
                summed = summed + jnp.einsum("nxyzi,io->nxyzo", window, weights_wide[9 * depth_x + 3 * depth_y + depth_z])
    result = (summed + channel_bias.astype(jnp.float32)) * occupied[..., None].astype(jnp.float32)
    return result.astype(jnp.bfloat16).reshape(block_count, BS, BS, BS * C)


def reference(features, occupancy, neighbors, face_lists, face_relays, send_slots, receive_order, weights, channel_bias):
    def masked_rows(index_x, index_y, chosen):
        blocks = jnp.take(features[index_x, index_y], chosen, axis=0)
        mask_words = jnp.take(occupancy[index_x, index_y], chosen, axis=0)
        return apply_mask(blocks, mask_words)

    def pool_y(index_x, index_y):
        own_rows = masked_rows(index_x, index_y, jnp.arange(HOME_SLOTS, dtype=jnp.int32))
        below = jnp.maximum(index_y - 1, 0)
        above = jnp.minimum(index_y + 1, N_GY - 1)
        lower = masked_rows(index_x, below, face_lists[index_x, below, FACE:]) * (index_y > 0).astype(own_rows.dtype)
        upper = masked_rows(index_x, above, face_lists[index_x, above, :FACE]) * (index_y < N_GY - 1).astype(own_rows.dtype)
        return jnp.concatenate([own_rows, lower, upper], axis=0)

    def device_result(index_x, index_y):
        mine = pool_y(index_x, index_y)
        left_x = jnp.maximum(index_x - 1, 0)
        right_x = jnp.minimum(index_x + 1, N_GX - 1)
        lower = jnp.take(pool_y(left_x, index_y), face_relays[left_x, index_y, FACE:], axis=0) * (index_x > 0).astype(mine.dtype)
        upper = jnp.take(pool_y(right_x, index_y), face_relays[right_x, index_y, :FACE], axis=0) * (index_x < N_GX - 1).astype(mine.dtype)
        empty_block = jnp.zeros((1,) + mine.shape[1:], mine.dtype)
        block_pool = jnp.concatenate([mine, lower, upper, empty_block], axis=0)
        tiles = assemble(block_pool, neighbors[index_x, index_y])
        occupied = unpack_bits(occupancy[index_x, index_y])
        return convolve(tiles, weights, channel_bias, occupied)

    def row_outputs(index_x):
        results = lax.map(lambda index_y: device_result(index_x, index_y), jnp.arange(N_GY, dtype=jnp.int32))
        orders = receive_order[index_x]
        source = (orders // PEER_SLOTS).astype(jnp.int32)
        item_index = (orders % PEER_SLOTS).astype(jnp.int32)
        target = jnp.arange(N_GY, dtype=jnp.int32)[:, None]
        held_slot = send_slots[index_x][source, target, item_index]
        return results[source, held_slot]

    return lax.map(row_outputs, jnp.arange(N_GX, dtype=jnp.int32))
```

```python
import functools

import jax
import jax.numpy as jnp
from jax import lax
from jax.experimental import pallas as pl
from jax.experimental.pallas import tpu as pltpu
from jax.sharding import PartitionSpec as P

C = 64
BS = 8
ROWS = BS * BS
LANES = BS * C
WORD_BITS = 21
GROUP = 4
K_BAND = (GROUP + 2) * C
N_BAND = GROUP * C
EXT = (BS + 2) * C
VMEM_LIMIT = 48 * 1024 * 1024

ANY = pl.BlockSpec(memory_space=pl.ANY)
SMEM = pl.BlockSpec(memory_space=pltpu.SMEM)
VMEM = pl.BlockSpec(memory_space=pltpu.VMEM)


def params():
    return pltpu.CompilerParams(vmem_limit_bytes=VMEM_LIMIT)


def voxel_ids(x):
    rows = lax.broadcasted_iota(jnp.int32, (BS, LANES), 0)
    lanes = lax.broadcasted_iota(jnp.int32, (BS, LANES), 1)
    return x * ROWS + rows * BS + lanes // C


def shift_amounts(x):
    v = voxel_ids(x)
    first = (x * ROWS) // WORD_BITS
    last = (x * ROWS + ROWS - 1) // WORD_BITS
    amounts = v - first * WORD_BITS
    for k in range(first + 1, last + 1):
        amounts = jnp.where(v >= k * WORD_BITS, v - k * WORD_BITS, amounts)
    return amounts


def plane_bits(occ_ref, slot, x, shifts):
    v = voxel_ids(x)
    first = (x * ROWS) // WORD_BITS
    last = (x * ROWS + ROWS - 1) // WORD_BITS
    words = jnp.full((BS, LANES), occ_ref[slot, first], jnp.int32)
    for k in range(first + 1, last + 1):
        words = jnp.where(v >= k * WORD_BITS, occ_ref[slot, k], words)
    return lax.shift_right_logical(words, shifts) & 1


def mask_block(occ_ref, slot, shift_ref, source, target):
    for i in range(BS // 2):
        bits = jnp.concatenate(
            [
                plane_bits(occ_ref, slot, x, shift_ref[x])
                for x in (2 * i, 2 * i + 1)
            ],
            axis=0,
        )
        rows = pl.ds(2 * BS * i, 2 * BS)
        values = source[rows, :].astype(jnp.float32)
        target[rows, :] = jnp.where(bits > 0, values, 0.0).astype(jnp.bfloat16)


def outgoing_kernel(lists_ref, occ_ref, feat_ref, low_ref, high_ref, held, shift_ref, sems):
    count = held.shape[0]
    width = count // 2
    copies = [
        pltpu.make_async_copy(feat_ref.at[lists_ref[t]], held.at[t], sems.at[t]) for t in range(count)
    ]
    for copy in copies:
        copy.start()
    for x in range(BS):
        shift_ref[x] = shift_amounts(x)
    for copy in copies:
        copy.wait()

    def body(t, carry):
        mask_block(occ_ref, lists_ref[t], shift_ref, held.at[t], low_ref.at[t])
        mask_block(occ_ref, lists_ref[t + width], shift_ref, held.at[t + width], high_ref.at[t])
        return carry

    lax.fori_loop(0, width, body, 0)


def masked_outgoing(face_lists, occupancy, features):
    count = face_lists.shape[0]
    half = jax.ShapeDtypeStruct((count // 2, ROWS, LANES), jnp.bfloat16)
    return pl.pallas_call(
        outgoing_kernel,
        out_shape=(half, half),
        in_specs=[SMEM, SMEM, ANY],
        out_specs=(VMEM, VMEM),
        scratch_shapes=[
            pltpu.VMEM((count, ROWS, LANES), jnp.bfloat16),
            pltpu.VMEM((BS, BS, LANES), jnp.int32),
            pltpu.SemaphoreType.DMA((count,)),
        ],
        compiler_params=params(),
        cost_estimate=pl.CostEstimate(flops=2000000, bytes_accessed=2 * count * ROWS * LANES * 2, transcendentals=0),
        name="mask_outgoing",
    )(face_lists, occupancy, features)


def mask_all_kernel(occ_ref, feat_ref, out_ref, shift_ref):
    per_step = feat_ref.shape[0]
    step = pl.program_id(0)

    @pl.when(step == 0)
    def _():
        for x in range(BS):
            shift_ref[x] = shift_amounts(x)

    def body(t, carry):
        mask_block(occ_ref, step * per_step + t, shift_ref, feat_ref.at[t], out_ref.at[t])
        return carry

    lax.fori_loop(0, per_step, body, 0)


def masked_all(occupancy, features):
    slots = features.shape[0]
    per_step = 8
    spec = pl.BlockSpec((per_step, ROWS, LANES), lambda i: (i, 0, 0))
    return pl.pallas_call(
        mask_all_kernel,
        grid=(slots // per_step,),
        out_shape=jax.ShapeDtypeStruct(features.shape, jnp.bfloat16),
        in_specs=[SMEM, spec],
        out_specs=spec,
        scratch_shapes=[pltpu.VMEM((BS, BS, LANES), jnp.int32)],
        compiler_params=params(),
        cost_estimate=pl.CostEstimate(flops=8000000, bytes_accessed=2 * slots * ROWS * LANES * 2, transcendentals=0),
        name="mask_held",
    )(occupancy, features)


def bands_kernel(weights_ref, out_ref):
    zeros = jnp.zeros((C, C), jnp.float32)
    for pair in range(9):
        taps = [weights_ref[3 * pair + c].astype(jnp.float32) for c in range(3)]
        for z_in in range(GROUP + 2):
            row = [taps[z_in - z_out] if 0 <= z_in - z_out <= 2 else zeros for z_out in range(GROUP)]
            out_ref[pair, pl.ds(z_in * C, C), :] = jnp.concatenate(row, axis=1).astype(jnp.bfloat16)


def banded(weights):
    return pl.pallas_call(
        bands_kernel,
        out_shape=jax.ShapeDtypeStruct((9, K_BAND, N_BAND), jnp.bfloat16),
        in_specs=[VMEM],
        out_specs=VMEM,
        compiler_params=params(),
        cost_estimate=pl.CostEstimate(flops=100000, bytes_accessed=4000000, transcendentals=0),
        name="band_weights",
    )(weights)


def relay_kernel(relays_ref, held_ref, low_ref, high_ref, out_low, out_high, sems):
    held = held_ref.shape[0]
    width = low_ref.shape[0]
    targets = [out_low.at[t] for t in range(width)] + [out_high.at[t] for t in range(width)]
    for t, target in enumerate(targets):
        index = relays_ref[t]

        @pl.when(index < held)
        def _():
            pltpu.make_async_copy(held_ref.at[index], target, sems.at[t]).start()

        @pl.when((index >= held) & (index < held + width))
        def _():
            pltpu.make_async_copy(low_ref.at[index - held], target, sems.at[t]).start()

        @pl.when(index >= held + width)
        def _():
            pltpu.make_async_copy(high_ref.at[index - held - width], target, sems.at[t]).start()

    for t, target in enumerate(targets):
        pltpu.make_async_copy(held_ref.at[0], target, sems.at[t]).wait()


def relayed(face_relays, held, low, high):
    half = jax.ShapeDtypeStruct(low.shape, jnp.bfloat16)
    count = face_relays.shape[0]
    return pl.pallas_call(
        relay_kernel,
        out_shape=(half, half),
        in_specs=[SMEM, ANY, ANY, ANY],
        out_specs=(ANY, ANY),
        scratch_shapes=[pltpu.SemaphoreType.DMA((count,))],
        compiler_params=params(),
        cost_estimate=pl.CostEstimate(flops=0, bytes_accessed=2 * count * ROWS * LANES * 2, transcendentals=0),
        name="gather_relays",
    )(face_relays, held, low, high)


def extended_plane(blocks, lane_low):
    below, own, above = blocks
    columns = [below] + [own[:, 128 * i : 128 * i + 128] for i in range(4)] + [above]
    turned = [pltpu.roll(column, C, 1) for column in columns]
    return [jnp.where(lane_low, turned[i], turned[i + 1]) for i in range(5)]


def conv_kernel(
    me_ref,
    slots_ref,
    occ_ref,
    neighbors_ref,
    bias_ref,
    bands_ref,
    held_ref,
    y_low_ref,
    y_high_ref,
    x_low_ref,
    x_high_ref,
    out_ref,
    pool,
    tiles,
    shift_ref,
    sems,
    *,
    distance,
):
    items = out_ref.shape[0]
    pairs = (items + 1) // 2
    held = held_ref.shape[0]
    width = y_low_ref.shape[0]
    parts = [held_ref, y_low_ref, y_high_ref, x_low_ref, x_high_ref]
    starts = [0, held, held + width, held + 2 * width, held + 3 * width]
    copies = [
        pltpu.make_async_copy(part, pool.at[pl.ds(start, part.shape[0])], sems.at[i])
        for i, (part, start) in enumerate(zip(parts, starts))
    ]
    for copy in copies:
        copy.start()
    pool[held + 4 * width] = jnp.zeros((ROWS, LANES), jnp.bfloat16)
    for x in range(BS):
        shift_ref[x] = shift_amounts(x)
    partner = me_ref[0] ^ distance
    for copy in copies:
        copy.wait()

    row_ids = lax.broadcasted_iota(jnp.int32, (BS, 128), 0)
    lane_low = lax.broadcasted_iota(jnp.int32, (2 * BS, 128), 1) < C
    is_last = row_ids == BS - 1
    is_first = row_ids == 0

    def slot_of(item):
        return jnp.maximum(slots_ref[partner, jnp.minimum(item, items - 1)], 0)

    def row_pair(slot, depth_x, depth_y, i):
        first = 9 * depth_x + 3 * depth_y
        rows = pl.ds(2 * BS * i, 2 * BS)
        below = pool[neighbors_ref[slot, first], rows, pl.ds(LANES - 128, 128)]
        own = pool[neighbors_ref[slot, first + 1], rows, :]
        above = pool[neighbors_ref[slot, first + 2], rows, pl.ds(0, 128)]
        return extended_plane([v.astype(jnp.float32) for v in (below, own, above)], lane_low)

    def build(pair, carry):
        slots = [slot_of(2 * pair), slot_of(2 * pair + 1)]
        for depth_x, i in ((0, 3), (1, 0), (1, 1), (1, 2), (1, 3), (2, 0)):
            rows = [[row_pair(slot, depth_x, depth_y, i) for depth_y in range(3)] for slot in slots]
            if depth_x == 0:
                planes = ((1, 0),)
            elif depth_x == 2:
                planes = ((0, BS + 1),)
            else:
                planes = ((0, 2 * i + 1), (1, 2 * i + 2))
            for half, plane in planes:
                cut = slice(half * BS, half * BS + BS)
                for column in range(5):
                    lanes = pl.ds(128 * column, 128)
                    shifted = ([], [], [])
                    for k in range(2):
                        before, own, after = (rows[k][depth_y][column][cut] for depth_y in range(3))
                        shifted[0].append(pltpu.roll(jnp.where(is_last, before, own), 1, 0))
                        shifted[1].append(own)
                        shifted[2].append(pltpu.roll(jnp.where(is_first, after, own), BS - 1, 0))
                    for depth_y in range(3):
                        tiles[depth_y, plane, pair, :, lanes] = jnp.concatenate(shifted[depth_y], axis=0).astype(
                            jnp.bfloat16
                        )
        return carry

    lax.fori_loop(0, pairs, build, 0)

    bias = bias_ref[...]
    for group in range(BS // GROUP):
        window = pl.ds(group * N_BAND, K_BAND)
        total = None
        for depth_x in range(3):
            for depth_y in range(3):
                left = tiles[depth_y, pl.ds(depth_x, BS), :, :, window].reshape(BS * pairs * 2 * BS, K_BAND)
                term = jnp.dot(left, bands_ref[3 * depth_x + depth_y], preferred_element_type=jnp.float32)
                total = term if total is None else total + term
        total = (total + bias).reshape(BS, pairs * 2, BS, N_BAND)
        for item in range(items):
            slot = slot_of(item)
            for i in range(BS // 2):
                parts = []
                for x in (2 * i, 2 * i + 1):
                    bits = plane_bits(occ_ref, slot, x, shift_ref[x])[:, group * N_BAND : group * N_BAND + N_BAND]
                    parts.append(jnp.where(bits > 0, total[x, item], 0.0))
                out_ref[item, pl.ds(2 * BS * i, 2 * BS), pl.ds(group * N_BAND, N_BAND)] = jnp.concatenate(
                    parts, axis=0
                ).astype(jnp.bfloat16)


def convolved(distance, me, send_slots, occupancy, neighbors, bias, bands, parts):
    items = send_slots.shape[1]
    pairs = (items + 1) // 2
    held = parts[0].shape[0]
    pool_blocks = sum(part.shape[0] for part in parts) + 1
    return pl.pallas_call(
        functools.partial(conv_kernel, distance=distance),
        out_shape=jax.ShapeDtypeStruct((items, ROWS, LANES), jnp.bfloat16),
        in_specs=[SMEM, SMEM, SMEM, SMEM, VMEM, VMEM] + [ANY] * 5,
        out_specs=VMEM,
        scratch_shapes=[
            pltpu.VMEM((pool_blocks, ROWS, LANES), jnp.bfloat16),
            pltpu.VMEM((3, BS + 2, pairs, 2 * BS, EXT), jnp.bfloat16),
            pltpu.VMEM((BS, BS, LANES), jnp.int32),
            pltpu.SemaphoreType.DMA((5,)),
        ],
        compiler_params=params(),
        cost_estimate=pl.CostEstimate(
            flops=2 * 9 * 2 * items * ROWS * K_BAND * N_BAND,
            bytes_accessed=(pool_blocks + items) * ROWS * LANES * 2 + 9 * K_BAND * N_BAND * 2,
            transcendentals=0,
        ),
        name="convolve_%d" % distance,
    )(me, send_slots, occupancy, neighbors, bias, bands, *parts)


def place_kernel(me_ref, order_ref, *refs):
    sems = refs[-1]
    out_ref = refs[-2]
    sources = refs[:-2]
    items = sources[0].shape[0]

    def body(r, carry):
        name = order_ref[r]
        distance = me_ref[0] ^ (name // items)
        for m, source in enumerate(sources):

            @pl.when(distance == m)
            def _():
                pltpu.make_async_copy(source.at[name % items], out_ref.at[r], sems.at[r]).start()

        return carry

    lax.fori_loop(0, out_ref.shape[0], body, 0)
    for r in range(out_ref.shape[0]):
        pltpu.make_async_copy(sources[0].at[0], out_ref.at[r], sems.at[r]).wait()


def placed(me, receive_order, arrived):
    count = receive_order.shape[0]
    return pl.pallas_call(
        place_kernel,
        out_shape=jax.ShapeDtypeStruct((count, ROWS, LANES), jnp.bfloat16),
        in_specs=[SMEM, SMEM] + [ANY] * len(arrived),
        out_specs=ANY,
        scratch_shapes=[pltpu.SemaphoreType.DMA((count,))],
        compiler_params=params(),
        cost_estimate=pl.CostEstimate(flops=0, bytes_accessed=2 * count * ROWS * LANES * 2, transcendentals=0),
        name="place_rows",
    )(me, receive_order, *arrived)


def both_ways(low, high, axis):
    ends = lax.axis_size(axis) - 1
    from_low = lax.ppermute(high, axis, [(i, i + 1) for i in range(ends)])
    from_high = lax.ppermute(low, axis, [(i + 1, i) for i in range(ends)])
    return from_low, from_high


def on_device(
    features,
    occupancy,
    neighbors,
    face_lists,
    face_relays,
    send_slots,
    receive_order,
    weights,
    channel_bias,
):
    slots = features.shape[2]
    blocks = features.reshape(slots, ROWS, LANES)
    words = occupancy[0, 0]
    me = lax.axis_index("gy").astype(jnp.int32).reshape(1)
    peers = lax.axis_size("gy")

    out_low, out_high = masked_outgoing(face_lists[0, 0], words, blocks)
    y_low, y_high = both_ways(out_low, out_high, "gy")
    held = masked_all(words, blocks)
    bands = banded(weights)
    bias = jnp.tile(channel_bias, GROUP).reshape(1, N_BAND)
    relay_low, relay_high = relayed(face_relays[0, 0], held, y_low, y_high)
    x_low, x_high = both_ways(relay_low, relay_high, "gx")

    parts = (held, y_low, y_high, x_low, x_high)
    arrived = [None] * peers
    far_first = [m for m in range(peers) if m >= peers // 2] + [m for m in reversed(range(peers // 2))]
    for m in far_first:
        result = convolved(m, me, send_slots[0, 0], words, neighbors[0, 0], bias, bands, parts)
        arrived[m] = lax.ppermute(result, "gy", [(d, d ^ m) for d in range(peers)]) if m else result
    output = placed(me, receive_order[0, 0], arrived)
    return output.reshape(1, 1, output.shape[0], BS, BS, LANES)


def solution(mesh):
    in_specs = (
        P("gx", "gy", None, None, None, None),
        P("gx", "gy", None, None),
        P("gx", "gy", None, None),
        P("gx", "gy", None),
        P("gx", "gy", None),
        P("gx", "gy", None, None),
        P("gx", "gy", None),
        P(),
        P(),
    )
    out_specs = P("gx", "gy", None, None, None, None)
    return jax.shard_map(
        on_device, mesh=mesh, in_specs=in_specs, out_specs=out_specs, check_vma=False
    )
```

```python
import functools

import jax
import jax.numpy as jnp
from jax import lax
from jax.experimental import pallas as pl
from jax.experimental.pallas import tpu as pltpu
from jax.sharding import PartitionSpec as P

C = 64
BS = 8
ROWS = BS * BS
LANES = BS * C
WORD_BITS = 21
GROUP = 4
K_BAND = (GROUP + 2) * C
N_BAND = GROUP * C
EXT = (BS + 2) * C
SHELL = (2 * BS, LANES + 6 * 128)
VMEM_LIMIT = 16 * 1024 * 1024
FIRST_LIMIT = 56 * 1024 * 1024

ANY = pl.BlockSpec(memory_space=pl.ANY)
SMEM = pl.BlockSpec(memory_space=pltpu.SMEM)
VMEM = pl.BlockSpec(memory_space=pltpu.VMEM)


def params():
    return pltpu.CompilerParams(vmem_limit_bytes=VMEM_LIMIT)


def voxel_ids(x):
    rows = lax.broadcasted_iota(jnp.int32, (BS, LANES), 0)
    lanes = lax.broadcasted_iota(jnp.int32, (BS, LANES), 1)
    return x * ROWS + rows * BS + lanes // C


def shift_amounts(x):
    v = voxel_ids(x)
    first = (x * ROWS) // WORD_BITS
    last = (x * ROWS + ROWS - 1) // WORD_BITS
    amounts = v - first * WORD_BITS
    for k in range(first + 1, last + 1):
        amounts = jnp.where(v >= k * WORD_BITS, v - k * WORD_BITS, amounts)
    return amounts


def plane_bits(occ_ref, slot, x, shifts):
    v = voxel_ids(x)
    first = (x * ROWS) // WORD_BITS
    last = (x * ROWS + ROWS - 1) // WORD_BITS
    words = jnp.full((BS, LANES), occ_ref[first, 0, slot], jnp.int32)
    for k in range(first + 1, last + 1):
        words = jnp.where(v >= k * WORD_BITS, occ_ref[k, 0, slot], words)
    return lax.shift_right_logical(words, shifts) & 1


def masked_planes(occ_ref, slot, shift_ref, source):
    planes = []
    for i in range(BS // 2):
        values = source[pl.ds(2 * BS * i, 2 * BS), :].astype(jnp.float32)
        for half in range(2):
            x = 2 * i + half
            bits = plane_bits(occ_ref, slot, x, shift_ref[x])
            planes.append(jnp.where(bits > 0, values[half * BS : half * BS + BS], 0.0))
    return planes


def store_pair(ref, lanes, first, second):
    ref[:, lanes] = jnp.concatenate([first, second], axis=0).astype(jnp.bfloat16)


def store_block(ref, planes):
    for i in range(BS // 2):
        rows = pl.ds(2 * BS * i, 2 * BS)
        ref[rows, :] = jnp.concatenate(planes[2 * i : 2 * i + 2], axis=0).astype(jnp.bfloat16)


def columns_of(plane):
    return [plane[:, 128 * i : 128 * i + 128] for i in range(LANES // 128)]


def tile_ids():
    rows = lax.broadcasted_iota(jnp.int32, (BS, 128), 0)
    lanes = lax.broadcasted_iota(jnp.int32, (BS, 128), 1)
    return rows, lanes


def pack_shell(ref, planes):
    rows, lanes = tile_ids()
    store_pair(ref, pl.ds(0, LANES), planes[0], planes[BS - 1])
    edges, ends = [], []
    for x in range(1, BS - 1):
        columns = columns_of(planes[x])
        edges.append(jnp.where(lanes < C, columns[0], columns[-1]))
        end = columns[0]
        for i, column in enumerate(columns):
            if i:
                end = jnp.where(rows == i, pltpu.roll(column, i, 0), end)
            end = jnp.where(rows == 4 + i, pltpu.roll(column, (i + 5) % BS, 0), end)
        ends.append(end)
    for k in range(3):
        store_pair(ref, pl.ds(LANES + 128 * k, 128), edges[2 * k], edges[2 * k + 1])
        store_pair(ref, pl.ds(LANES + 128 * (3 + k), 128), ends[2 * k], ends[2 * k + 1])


def unpack_shell(ref, packed):
    rows, _ = tile_ids()
    outer = packed[:, pl.ds(0, LANES)].astype(jnp.float32)
    planes = [None] * BS
    planes[0], planes[BS - 1] = outer[:BS], outer[BS:]
    for k in range(3):
        edges = packed[:, pl.ds(LANES + 128 * k, 128)].astype(jnp.float32)
        ends = packed[:, pl.ds(LANES + 128 * (3 + k), 128)].astype(jnp.float32)
        for half in range(2):
            cut = slice(half * BS, half * BS + BS)
            edge, end = edges[cut], ends[cut]
            columns = []
            for i in range(4):
                first = pltpu.roll(end, (BS - i) % BS, 0) if i else end
                last = pltpu.roll(end, (3 - i) % BS, 0) if i != 3 else end
                columns.append(jnp.where(rows == 0, first, jnp.where(rows == BS - 1, last, edge)))
            planes[2 * k + 1 + half] = jnp.concatenate(columns, axis=1)
    store_block(ref, planes)


def outgoing_kernel(lists_ref, occ_ref, feat_ref, low_ref, high_ref, held, shift_ref, sems):
    count = held.shape[0]
    width = count // 2
    copies = [
        pltpu.make_async_copy(feat_ref.at[lists_ref[t]], held.at[t], sems.at[t]) for t in range(count)
    ]
    for copy in copies:
        copy.start()
    for x in range(BS):
        shift_ref[x] = shift_amounts(x)
    for copy in copies:
        copy.wait()

    def body(t, carry):
        pack_shell(low_ref.at[t], masked_planes(occ_ref, lists_ref[t], shift_ref, held.at[t]))
        pack_shell(
            high_ref.at[t], masked_planes(occ_ref, lists_ref[t + width], shift_ref, held.at[t + width])
        )
        return carry

    lax.fori_loop(0, width, body, 0)


def masked_outgoing(face_lists, occupancy, features):
    count = face_lists.shape[0]
    half = jax.ShapeDtypeStruct((count // 2,) + SHELL, jnp.bfloat16)
    return pl.pallas_call(
        outgoing_kernel,
        out_shape=(half, half),
        in_specs=[SMEM, SMEM, ANY],
        out_specs=(VMEM, VMEM),
        scratch_shapes=[
            pltpu.VMEM((count, ROWS, LANES), jnp.bfloat16),
            pltpu.VMEM((BS, BS, LANES), jnp.int32),
            pltpu.SemaphoreType.DMA((count,)),
        ],
        compiler_params=pltpu.CompilerParams(vmem_limit_bytes=FIRST_LIMIT),
        cost_estimate=pl.CostEstimate(flops=2000000, bytes_accessed=2 * count * ROWS * LANES * 2, transcendentals=0),
        name="mask_outgoing",
    )(face_lists, occupancy, features)


def mask_all_kernel(occ_ref, feat_ref, pool_ref, shells_ref, shift_ref):
    for x in range(BS):
        shift_ref[x] = shift_amounts(x)
    pool_ref[pool_ref.shape[0] - 1] = jnp.zeros((ROWS, LANES), jnp.bfloat16)

    def body(t, carry):
        planes = masked_planes(occ_ref, t, shift_ref, feat_ref.at[t])
        store_block(pool_ref.at[t], planes)
        pack_shell(shells_ref.at[t], planes)
        return carry

    lax.fori_loop(0, feat_ref.shape[0], body, 0)


def masked_all(occupancy, features, pool_blocks):
    slots = features.shape[0]
    return pl.pallas_call(
        mask_all_kernel,
        out_shape=(
            jax.ShapeDtypeStruct((pool_blocks, ROWS, LANES), jnp.bfloat16),
            jax.ShapeDtypeStruct((slots,) + SHELL, jnp.bfloat16),
        ),
        in_specs=[SMEM, VMEM],
        out_specs=(VMEM, VMEM),
        scratch_shapes=[pltpu.VMEM((BS, BS, LANES), jnp.int32)],
        compiler_params=params(),
        cost_estimate=pl.CostEstimate(flops=8000000, bytes_accessed=3 * slots * ROWS * LANES * 2, transcendentals=0),
        name="mask_held",
    )(occupancy, features)


def unpack_kernel(pool_in, low_ref, high_ref, pool_ref, *, start):
    width = low_ref.shape[0]

    def body(t, carry):
        unpack_shell(pool_ref.at[start + t], low_ref.at[t])
        unpack_shell(pool_ref.at[start + width + t], high_ref.at[t])
        return carry

    lax.fori_loop(0, width, body, 0)


def unpacked(pool, low, high, start):
    return pl.pallas_call(
        functools.partial(unpack_kernel, start=start),
        out_shape=jax.ShapeDtypeStruct(pool.shape, pool.dtype),
        in_specs=[VMEM, VMEM, VMEM],
        out_specs=VMEM,
        input_output_aliases={0: 0},
        compiler_params=params(),
        cost_estimate=pl.CostEstimate(flops=100000, bytes_accessed=1000000, transcendentals=0),
        name="unpack_%d" % start,
    )(pool, low, high)


def bands_kernel(weights_ref, out_ref):
    zeros = jnp.zeros((C, C), jnp.float32)
    for pair in range(9):
        taps = [weights_ref[3 * pair + c].astype(jnp.float32) for c in range(3)]
        for z_in in range(GROUP + 2):
            row = [taps[z_in - z_out] if 0 <= z_in - z_out <= 2 else zeros for z_out in range(GROUP)]
            out_ref[pair, pl.ds(z_in * C, C), :] = jnp.concatenate(row, axis=1).astype(jnp.bfloat16)


def banded(weights):
    return pl.pallas_call(
        bands_kernel,
        out_shape=jax.ShapeDtypeStruct((9, K_BAND, N_BAND), jnp.bfloat16),
        in_specs=[VMEM],
        out_specs=VMEM,
        compiler_params=params(),
        cost_estimate=pl.CostEstimate(flops=100000, bytes_accessed=4000000, transcendentals=0),
        name="band_weights",
    )(weights)


def relay_kernel(relays_ref, held_ref, low_ref, high_ref, out_low, out_high, sems):
    held = held_ref.shape[0]
    width = low_ref.shape[0]
    targets = [out_low.at[t] for t in range(width)] + [out_high.at[t] for t in range(width)]
    for t, target in enumerate(targets):
        index = relays_ref[t]

        @pl.when(index < held)
        def _():
            pltpu.make_async_copy(held_ref.at[index], target, sems.at[t]).start()

        @pl.when((index >= held) & (index < held + width))
        def _():
            pltpu.make_async_copy(low_ref.at[index - held], target, sems.at[t]).start()

        @pl.when(index >= held + width)
        def _():
            pltpu.make_async_copy(high_ref.at[index - held - width], target, sems.at[t]).start()

    for t, target in enumerate(targets):
        pltpu.make_async_copy(held_ref.at[0], target, sems.at[t]).wait()


def relayed(face_relays, held, low, high):
    half = jax.ShapeDtypeStruct(low.shape, jnp.bfloat16)
    count = face_relays.shape[0]
    return pl.pallas_call(
        relay_kernel,
        out_shape=(half, half),
        in_specs=[SMEM, ANY, ANY, ANY],
        out_specs=(ANY, ANY),
        scratch_shapes=[pltpu.SemaphoreType.DMA((count,))],
        compiler_params=params(),
        cost_estimate=pl.CostEstimate(flops=0, bytes_accessed=2 * count * SHELL[0] * SHELL[1] * 2, transcendentals=0),
        name="gather_relays",
    )(face_relays, held, low, high)


def extended_plane(blocks, lane_low):
    below, own, above = blocks
    columns = [below] + [own[:, 128 * i : 128 * i + 128] for i in range(4)] + [above]
    turned = [pltpu.roll(column, C, 1) for column in columns]
    return [jnp.where(lane_low, turned[i], turned[i + 1]) for i in range(5)]


def conv_kernel(
    me_ref,
    slots_ref,
    occ_ref,
    neighbors_ref,
    bias_ref,
    bands_ref,
    pool,
    earlier_ref,
    out_ref,
    tiles,
    shift_ref,
    *,
    distance,
):
    items = out_ref.shape[0]
    pairs = (items + 1) // 2
    for x in range(BS):
        shift_ref[x] = shift_amounts(x)
    partner = me_ref[0] ^ distance

    row_ids = lax.broadcasted_iota(jnp.int32, (BS, 128), 0)
    lane_low = lax.broadcasted_iota(jnp.int32, (2 * BS, 128), 1) < C
    is_last = row_ids == BS - 1
    is_first = row_ids == 0

    def slot_of(item):
        return jnp.maximum(slots_ref[jnp.minimum(item, items - 1), partner], 0)

    def row_pair(slot, depth_x, depth_y, i):
        first = 9 * depth_x + 3 * depth_y
        rows = pl.ds(2 * BS * i, 2 * BS)
        below = pool[neighbors_ref[first, 0, slot], rows, pl.ds(LANES - 128, 128)]
        own = pool[neighbors_ref[first + 1, 0, slot], rows, :]
        above = pool[neighbors_ref[first + 2, 0, slot], rows, pl.ds(0, 128)]
        return extended_plane([v.astype(jnp.float32) for v in (below, own, above)], lane_low)

    def build(pair, carry):
        slots = [slot_of(2 * pair), slot_of(2 * pair + 1)]
        for depth_x, i in ((0, 3), (1, 0), (1, 1), (1, 2), (1, 3), (2, 0)):
            rows = [[row_pair(slot, depth_x, depth_y, i) for depth_y in range(3)] for slot in slots]
            if depth_x == 0:
                planes = ((1, 0),)
            elif depth_x == 2:
                planes = ((0, BS + 1),)
            else:
                planes = ((0, 2 * i + 1), (1, 2 * i + 2))
            for half, plane in planes:
                cut = slice(half * BS, half * BS + BS)
                for column in range(5):
                    lanes = pl.ds(128 * column, 128)
                    shifted = ([], [], [])
                    for k in range(2):
                        before, own, after = (rows[k][depth_y][column][cut] for depth_y in range(3))
                        shifted[0].append(pltpu.roll(jnp.where(is_last, before, own), 1, 0))
                        shifted[1].append(own)
                        shifted[2].append(pltpu.roll(jnp.where(is_first, after, own), BS - 1, 0))
                    for depth_y in range(3):
                        tiles[depth_y, plane, pair, :, lanes] = jnp.concatenate(shifted[depth_y], axis=0).astype(
                            jnp.bfloat16
                        )
        return carry

    lax.fori_loop(0, pairs, build, 0)

    bias = bias_ref[...]
    for group in range(BS // GROUP):
        window = pl.ds(group * N_BAND, K_BAND)
        total = None
        for depth_x in range(3):
            for depth_y in range(3):
                left = tiles[depth_y, pl.ds(depth_x, BS), :, :, window].reshape(BS * pairs * 2 * BS, K_BAND)
                term = jnp.dot(left, bands_ref[3 * depth_x + depth_y], preferred_element_type=jnp.float32)
                total = term if total is None else total + term
        total = (total + bias).reshape(BS, pairs * 2, BS, N_BAND)
        for item in range(items):
            slot = slot_of(item)
            for i in range(BS // 2):
                parts = []
                for x in (2 * i, 2 * i + 1):
                    bits = plane_bits(occ_ref, slot, x, shift_ref[x])[:, group * N_BAND : group * N_BAND + N_BAND]
                    parts.append(jnp.where(bits > 0, total[x, item], 0.0))
                out_ref[item, pl.ds(2 * BS * i, 2 * BS), pl.ds(group * N_BAND, N_BAND)] = jnp.concatenate(
                    parts, axis=0
                ).astype(jnp.bfloat16)


def convolved(distance, me, send_slots, occupancy, neighbors, bias, bands, pool, earlier):
    items = send_slots.shape[0]
    pairs = (items + 1) // 2
    return pl.pallas_call(
        functools.partial(conv_kernel, distance=distance),
        out_shape=jax.ShapeDtypeStruct((items, ROWS, LANES), jnp.bfloat16),
        in_specs=[SMEM, SMEM, SMEM, SMEM, VMEM, VMEM, VMEM, ANY],
        out_specs=VMEM,
        scratch_shapes=[
            pltpu.VMEM((3, BS + 2, pairs, 2 * BS, EXT), jnp.bfloat16),
            pltpu.VMEM((BS, BS, LANES), jnp.int32),
        ],
        compiler_params=params(),
        cost_estimate=pl.CostEstimate(
            flops=2 * 9 * 2 * items * ROWS * K_BAND * N_BAND,
            bytes_accessed=(27 + items) * ROWS * LANES * 2 + 9 * K_BAND * N_BAND * 2,
            transcendentals=0,
        ),
        name="convolve_%d" % distance,
    )(me, send_slots, occupancy, neighbors, bias, bands, pool, earlier)


def place_kernel(me_ref, order_ref, *refs, distances):
    out_ref, sems = refs[-2:]
    sources = refs[: len(distances)]
    items = sources[0].shape[0]
    names = [order_ref[r] for r in range(out_ref.shape[0])]

    def each(act):
        for distance, source in zip(distances, sources):
            peer = me_ref[0] ^ distance
            for r, name in enumerate(names):

                @pl.when(name // items == peer)
                def _():
                    act(pltpu.make_async_copy(source.at[name % items], out_ref.at[r], sems.at[r]))

    each(lambda copy: copy.start())
    each(lambda copy: copy.wait())


def placed(distances, me, receive_order, arrived, output):
    count = receive_order.shape[0]
    filled = () if output is None else (output,)
    return pl.pallas_call(
        functools.partial(place_kernel, distances=distances),
        out_shape=jax.ShapeDtypeStruct((count, ROWS, LANES), jnp.bfloat16),
        in_specs=[SMEM, SMEM] + [ANY] * (len(distances) + len(filled)),
        out_specs=ANY,
        scratch_shapes=[pltpu.SemaphoreType.DMA((count,))],
        input_output_aliases={2 + len(distances): 0} if filled else {},
        compiler_params=params(),
        cost_estimate=pl.CostEstimate(flops=0, bytes_accessed=8 * ROWS * LANES * 2, transcendentals=0),
        name="place_%d" % distances[0],
    )(me, receive_order, *[arrived[m] for m in distances], *filled)


def both_ways(low, high, axis):
    ends = lax.axis_size(axis) - 1
    from_low = lax.ppermute(high, axis, [(i, i + 1) for i in range(ends)])
    from_high = lax.ppermute(low, axis, [(i + 1, i) for i in range(ends)])
    return from_low, from_high


def sending_order(peers):
    far = list(range(peers // 2, peers))
    near = list(reversed(range(1, peers // 2)))
    return far[:1] + near[:1] + far[1:2] + near[1:] + far[2:]


def on_device(
    features,
    occupancy,
    neighbors,
    face_lists,
    face_relays,
    send_slots,
    receive_order,
    weights,
    channel_bias,
):
    slots = features.shape[2]
    blocks = features.reshape(slots, ROWS, LANES)
    words = jnp.transpose(occupancy[0], (2, 0, 1))
    table = jnp.transpose(neighbors[0], (2, 0, 1))
    listed = jnp.transpose(send_slots[0, 0])
    me = lax.axis_index("gy").astype(jnp.int32).reshape(1)
    peers = lax.axis_size("gy")
    faces = face_lists.shape[-1]

    out_low, out_high = masked_outgoing(face_lists[0, 0], words, blocks)
    y_low, y_high = both_ways(out_low, out_high, "gy")
    pool, shells = masked_all(words, blocks, slots + 2 * faces + 1)
    bands = banded(weights)
    bias = jnp.tile(channel_bias, GROUP).reshape(1, N_BAND)
    relay_low, relay_high = relayed(face_relays[0, 0], shells, y_low, y_high)
    x_low, x_high = both_ways(relay_low, relay_high, "gx")
    pool = unpacked(pool, y_low, y_high, slots)
    pool = unpacked(pool, x_low, x_high, slots + faces)

    result, output = bias, None
    arrived = {}
    for m in sending_order(peers):
        result = convolved(m, me, listed, words, table, bias, bands, pool, result)
        arrived[m] = lax.ppermute(result, "gy", [(d, d ^ m) for d in range(peers)])
    arrived[0] = convolved(0, me, listed, words, table, bias, bands, pool, result)
    for m in [0] + sending_order(peers):
        output = placed((m,), me, receive_order[0, 0], arrived, output)
    return output.reshape(1, 1, output.shape[0], BS, BS, LANES)


def solution(mesh):
    in_specs = (
        P("gx", "gy", None, None, None, None),
        P("gx", "gy", None, None),
        P("gx", "gy", None, None),
        P("gx", "gy", None),
        P("gx", "gy", None),
        P("gx", "gy", None, None),
        P("gx", "gy", None),
        P(),
        P(),
    )
    out_specs = P("gx", "gy", None, None, None, None)
    return jax.shard_map(
        on_device, mesh=mesh, in_specs=in_specs, out_specs=out_specs, check_vma=False
    )
```

```python
import functools

import jax
import jax.numpy as jnp
from jax import lax
from jax.experimental import pallas as pl
from jax.experimental.pallas import tpu as pltpu
from jax.sharding import PartitionSpec as P

C = 64
BS = 8
ROWS = BS * BS
LANES = BS * C
WORD_BITS = 21
GROUP = 4
K_BAND = (GROUP + 2) * C
N_BAND = GROUP * C
EXT = (BS + 2) * C
SHELL = (2 * BS, LANES + 6 * 128)
VMEM_LIMIT = 16 * 1024 * 1024
FIRST_LIMIT = 56 * 1024 * 1024

LITTLE = pl.CostEstimate(flops=1, bytes_accessed=1, transcendentals=0)

ANY = pl.BlockSpec(memory_space=pl.ANY)
HBM = pl.BlockSpec(memory_space=pltpu.HBM)
SMEM = pl.BlockSpec(memory_space=pltpu.SMEM)
VMEM = pl.BlockSpec(memory_space=pltpu.VMEM)


def params():
    return pltpu.CompilerParams(vmem_limit_bytes=VMEM_LIMIT)


def voxel_ids(x):
    rows = lax.broadcasted_iota(jnp.int32, (BS, LANES), 0)
    lanes = lax.broadcasted_iota(jnp.int32, (BS, LANES), 1)
    return x * ROWS + rows * BS + lanes // C


def shift_amounts(x):
    v = voxel_ids(x)
    first = (x * ROWS) // WORD_BITS
    last = (x * ROWS + ROWS - 1) // WORD_BITS
    amounts = v - first * WORD_BITS
    for k in range(first + 1, last + 1):
        amounts = jnp.where(v >= k * WORD_BITS, v - k * WORD_BITS, amounts)
    return amounts


def plane_bits(occ_ref, slot, x, shifts):
    v = voxel_ids(x)
    first = (x * ROWS) // WORD_BITS
    last = (x * ROWS + ROWS - 1) // WORD_BITS
    words = jnp.full((BS, LANES), occ_ref[first, 0, slot], jnp.int32)
    for k in range(first + 1, last + 1):
        words = jnp.where(v >= k * WORD_BITS, occ_ref[k, 0, slot], words)
    return lax.shift_right_logical(words, shifts) & 1


def masked_planes(occ_ref, slot, shift_ref, source):
    planes = []
    for i in range(BS // 2):
        values = source[pl.ds(2 * BS * i, 2 * BS), :].astype(jnp.float32)
        for half in range(2):
            x = 2 * i + half
            bits = plane_bits(occ_ref, slot, x, shift_ref[x])
            planes.append(jnp.where(bits > 0, values[half * BS : half * BS + BS], 0.0))
    return planes


def store_pair(ref, lanes, first, second):
    ref[:, lanes] = jnp.concatenate([first, second], axis=0).astype(jnp.bfloat16)


def store_block(ref, planes):
    for i in range(BS // 2):
        rows = pl.ds(2 * BS * i, 2 * BS)
        ref[rows, :] = jnp.concatenate(planes[2 * i : 2 * i + 2], axis=0).astype(jnp.bfloat16)


def columns_of(plane):
    return [plane[:, 128 * i : 128 * i + 128] for i in range(LANES // 128)]


def tile_ids():
    rows = lax.broadcasted_iota(jnp.int32, (BS, 128), 0)
    lanes = lax.broadcasted_iota(jnp.int32, (BS, 128), 1)
    return rows, lanes


def pack_shell(ref, planes):
    rows, lanes = tile_ids()
    store_pair(ref, pl.ds(0, LANES), planes[0], planes[BS - 1])
    edges, ends = [], []
    for x in range(1, BS - 1):
        columns = columns_of(planes[x])
        edges.append(jnp.where(lanes < C, columns[0], columns[-1]))
        end = columns[0]
        for i, column in enumerate(columns):
            if i:
                end = jnp.where(rows == i, pltpu.roll(column, i, 0), end)
            end = jnp.where(rows == 4 + i, pltpu.roll(column, (i + 5) % BS, 0), end)
        ends.append(end)
    for k in range(3):
        store_pair(ref, pl.ds(LANES + 128 * k, 128), edges[2 * k], edges[2 * k + 1])
        store_pair(ref, pl.ds(LANES + 128 * (3 + k), 128), ends[2 * k], ends[2 * k + 1])


def unpack_shell(ref, packed):
    rows, _ = tile_ids()
    outer = packed[:, pl.ds(0, LANES)].astype(jnp.float32)
    planes = [None] * BS
    planes[0], planes[BS - 1] = outer[:BS], outer[BS:]
    for k in range(3):
        edges = packed[:, pl.ds(LANES + 128 * k, 128)].astype(jnp.float32)
        ends = packed[:, pl.ds(LANES + 128 * (3 + k), 128)].astype(jnp.float32)
        for half in range(2):
            cut = slice(half * BS, half * BS + BS)
            edge, end = edges[cut], ends[cut]
            columns = []
            for i in range(4):
                first = pltpu.roll(end, (BS - i) % BS, 0) if i else end
                last = pltpu.roll(end, (3 - i) % BS, 0) if i != 3 else end
                columns.append(jnp.where(rows == 0, first, jnp.where(rows == BS - 1, last, edge)))
            planes[2 * k + 1 + half] = jnp.concatenate(columns, axis=1)
    store_block(ref, planes)


def upper_first(axis):
    return lax.axis_index(axis) % 2 == 0


def partner_offset(axis, width):
    return jnp.where(upper_first(axis), width, 0)


def outgoing_kernel(lists_ref, words_ref, feat_ref, *refs, axis):
    partner_ref, other_ref, held, shift_ref, lists, words, list_sems, sems = refs[-8:]
    slots = feat_ref.shape[0]
    width = partner_ref.shape[0]
    lists_in = pltpu.make_async_copy(lists_ref, lists, list_sems.at[0])
    words_in = pltpu.make_async_copy(words_ref, words, list_sems.at[1])
    lists_in.start()
    words_in.start()
    lists_in.wait()
    offset = partner_offset(axis, width)
    jobs = []
    for target, start in ((partner_ref, offset), (other_ref, width - offset)):
        for t in range(width):
            name = lists[0, 0, start + t]
            k = len(jobs)
            copy_in = pltpu.make_async_copy(feat_ref.at[jnp.minimum(name, slots - 1)], held.at[k], sems.at[k])
            copy_in.start()
            jobs.append((copy_in, name, target.at[t]))
    for x in range(BS):
        shift_ref[x] = shift_amounts(x)
    words_in.wait()
    for k, (copy_in, name, target) in enumerate(jobs):
        copy_in.wait()

        @pl.when(name < slots)
        def _():
            pack_shell(target, masked_planes(words, name, shift_ref, held.at[k]))


def masked_outgoing(lists, occupancy, features, axis, after=()):
    count = lists.shape[-1]
    half = jax.ShapeDtypeStruct((count // 2,) + SHELL, jnp.bfloat16)
    return pl.pallas_call(
        functools.partial(outgoing_kernel, axis=axis),
        out_shape=(half, half),
        in_specs=[HBM, HBM, HBM] + [ANY] * len(after),
        out_specs=(VMEM, VMEM),
        scratch_shapes=[
            pltpu.VMEM((count, ROWS, LANES), jnp.bfloat16),
            pltpu.VMEM((BS, BS, LANES), jnp.int32),
            pltpu.SMEM(lists.shape, jnp.int32),
            pltpu.SMEM(occupancy.shape, jnp.int32),
            pltpu.SemaphoreType.DMA((2,)),
            pltpu.SemaphoreType.DMA((count,)),
        ],
        compiler_params=pltpu.CompilerParams(vmem_limit_bytes=FIRST_LIMIT),
        cost_estimate=pl.CostEstimate(flops=2000000, bytes_accessed=2 * count * ROWS * LANES * 2, transcendentals=0),
        name="mask_outgoing_" + axis,
    )(lists, occupancy, features, *after)


def unpack_neighbors(pool_ref, start, axis, partner_ref, other_ref):
    width = partner_ref.shape[0]
    offset = partner_offset(axis, width)
    for t in range(width):
        unpack_shell(pool_ref.at[start + offset + t], partner_ref.at[t])
        unpack_shell(pool_ref.at[start + width - offset + t], other_ref.at[t])


def mask_all_kernel(occ_ref, feat_ref, partner_ref, other_ref, earlier_ref, pool_ref, shift_ref):
    slots = feat_ref.shape[0]
    for x in range(BS):
        shift_ref[x] = shift_amounts(x)
    pool_ref[pool_ref.shape[0] - 1] = jnp.zeros((ROWS, LANES), jnp.bfloat16)

    def body(t, carry):
        store_block(pool_ref.at[t], masked_planes(occ_ref, t, shift_ref, feat_ref.at[t]))
        return carry

    lax.fori_loop(0, slots, body, 0)
    unpack_neighbors(pool_ref, slots, "gy", partner_ref, other_ref)


def masked_all(occupancy, features, partner, other, pool_blocks, earlier):
    slots = features.shape[0]
    return pl.pallas_call(
        mask_all_kernel,
        out_shape=jax.ShapeDtypeStruct((pool_blocks, ROWS, LANES), jnp.bfloat16),
        in_specs=[SMEM, VMEM, VMEM, VMEM, ANY],
        out_specs=VMEM,
        scratch_shapes=[pltpu.VMEM((BS, BS, LANES), jnp.int32)],
        compiler_params=params(),
        cost_estimate=pl.CostEstimate(flops=8000000, bytes_accessed=3 * slots * ROWS * LANES * 2, transcendentals=0),
        name="mask_held",
    )(occupancy, features, partner, other, earlier)


def bands_kernel(weights_ref, earlier_ref, out_ref):
    zeros = jnp.zeros((C, C), jnp.float32)
    for pair in range(9):
        taps = [weights_ref[3 * pair + c].astype(jnp.float32) for c in range(3)]
        for z_in in range(GROUP + 2):
            row = [taps[z_in - z_out] if 0 <= z_in - z_out <= 2 else zeros for z_out in range(GROUP)]
            out_ref[pair, pl.ds(z_in * C, C), :] = jnp.concatenate(row, axis=1).astype(jnp.bfloat16)


def banded(weights, earlier):
    return pl.pallas_call(
        bands_kernel,
        out_shape=jax.ShapeDtypeStruct((9, K_BAND, N_BAND), jnp.bfloat16),
        in_specs=[VMEM, ANY],
        out_specs=VMEM,
        compiler_params=params(),
        cost_estimate=pl.CostEstimate(flops=100000, bytes_accessed=4000000, transcendentals=0),
        name="band_weights",
    )(weights, earlier)


def relay_kernel(relays_ref, partner_ref, other_ref, own_partner, own_other, out_partner, out_other, sems, *, slots):
    width = partner_ref.shape[0]
    offset = partner_offset("gx", width)

    def each(act):
        for part, (start, out) in enumerate(((offset, out_partner), (width - offset, out_other))):
            for t in range(width):
                index = relays_ref[0, 0, start + t] - slots
                from_partner = (index >= width) == upper_first("gy")
                place = index % width
                sem = sems.at[part * width + t]

                @pl.when((index >= 0) & from_partner)
                def _():
                    act(pltpu.make_async_copy(partner_ref.at[place], out.at[t], sem))

                @pl.when((index >= 0) & jnp.logical_not(from_partner))
                def _():
                    act(pltpu.make_async_copy(other_ref.at[place], out.at[t], sem))

    each(lambda copy: copy.start())
    each(lambda copy: copy.wait())


def relayed(face_relays, partner, other, own_partner, own_other, slots):
    half = jax.ShapeDtypeStruct(partner.shape, jnp.bfloat16)
    count = face_relays.shape[-1]
    return pl.pallas_call(
        functools.partial(relay_kernel, slots=slots),
        out_shape=(half, half),
        in_specs=[SMEM, ANY, ANY, ANY, ANY],
        out_specs=(ANY, ANY),
        scratch_shapes=[pltpu.SemaphoreType.DMA((count,))],
        input_output_aliases={3: 0, 4: 1},
        compiler_params=params(),
        cost_estimate=pl.CostEstimate(flops=0, bytes_accessed=2 * count * SHELL[0] * SHELL[1] * 2, transcendentals=0),
        name="gather_relays",
    )(face_relays, partner, other, own_partner, own_other)


def extended_plane(blocks, lane_low):
    below, own, above = blocks
    columns = [below] + [own[:, 128 * i : 128 * i + 128] for i in range(4)] + [above]
    turned = [pltpu.roll(column, C, 1) for column in columns]
    return [jnp.where(lane_low, turned[i], turned[i + 1]) for i in range(5)]


def conv_kernel(sent_ref, table_ref, bias_ref, bands_ref, pool_ref, *refs, jobs, start, waits):
    refs = list(refs)
    shift_ref, tiles = refs.pop(), refs.pop()
    del refs[:waits]
    if start is None:
        pool = pool_ref
    else:
        pool = refs.pop()
        unpack_neighbors(pool, start, "gx", refs.pop(0), refs.pop(0))
    (out_ref,) = refs
    items = len(jobs)
    pairs = (items + 1) // 2
    for x in range(BS):
        shift_ref[x] = shift_amounts(x)
    me = lax.axis_index("gy")
    offsets = table_ref.shape[0] - 27
    slots = [jnp.maximum(sent_ref[item, me ^ distance], 0) for distance, item in jobs]
    slots = slots + slots[-1:] * (2 * pairs - items)

    row_ids = lax.broadcasted_iota(jnp.int32, (BS, 128), 0)
    lane_low = lax.broadcasted_iota(jnp.int32, (2 * BS, 128), 1) < C
    is_last = row_ids == BS - 1
    is_first = row_ids == 0

    def row_pair(slot, depth_x, depth_y, i):
        row = offsets + 9 * depth_x + 3 * depth_y
        rows = pl.ds(2 * BS * i, 2 * BS)
        below = pool[table_ref[row, 0, slot], rows, pl.ds(LANES - 128, 128)]
        own = pool[table_ref[row + 1, 0, slot], rows, :]
        above = pool[table_ref[row + 2, 0, slot], rows, pl.ds(0, 128)]
        return extended_plane([v.astype(jnp.float32) for v in (below, own, above)], lane_low)

    def build(pair, both):
        for depth_x, i in ((0, 3), (1, 0), (1, 1), (1, 2), (1, 3), (2, 0)):
            rows = [[row_pair(slot, depth_x, depth_y, i) for depth_y in range(3)] for slot in both]
            if depth_x == 0:
                planes = ((1, 0),)
            elif depth_x == 2:
                planes = ((0, BS + 1),)
            else:
                planes = ((0, 2 * i + 1), (1, 2 * i + 2))
            for half, plane in planes:
                cut = slice(half * BS, half * BS + BS)
                for column in range(5):
                    lanes = pl.ds(128 * column, 128)
                    shifted = ([], [], [])
                    for k in range(2):
                        before, own, after = (rows[k][depth_y][column][cut] for depth_y in range(3))
                        shifted[0].append(pltpu.roll(jnp.where(is_last, before, own), 1, 0))
                        shifted[1].append(own)
                        shifted[2].append(pltpu.roll(jnp.where(is_first, after, own), BS - 1, 0))
                    for depth_y in range(3):
                        tiles[depth_y, plane, pair, :, lanes] = jnp.concatenate(shifted[depth_y], axis=0).astype(
                            jnp.bfloat16
                        )

    for pair in range(pairs):
        build(pair, slots[2 * pair : 2 * pair + 2])

    bias = bias_ref[...]
    for group in range(BS // GROUP):
        window = pl.ds(group * N_BAND, K_BAND)
        total = None
        for depth_x in range(3):
            for depth_y in range(3):
                left = tiles[depth_y, pl.ds(depth_x, BS), :, :, window].reshape(BS * pairs * 2 * BS, K_BAND)
                term = jnp.dot(left, bands_ref[3 * depth_x + depth_y], preferred_element_type=jnp.float32)
                total = term if total is None else total + term
        total = (total + bias).reshape(BS, pairs * 2, BS, N_BAND)
        for item in range(items):
            slot = slots[item]
            for i in range(BS // 2):
                parts = []
                for x in (2 * i, 2 * i + 1):
                    bits = plane_bits(table_ref, slot, x, shift_ref[x])[:, group * N_BAND : group * N_BAND + N_BAND]
                    parts.append(jnp.where(bits > 0, total[x, item], 0.0))
                out_ref[item, pl.ds(2 * BS * i, 2 * BS), pl.ds(group * N_BAND, N_BAND)] = jnp.concatenate(
                    parts, axis=0
                ).astype(jnp.bfloat16)


def convolved(jobs, tables, bias, bands, pool, after, shells=(), start=None):
    pairs = (len(jobs) + 1) // 2
    out_shape = [jax.ShapeDtypeStruct((len(jobs), ROWS, LANES), jnp.bfloat16)]
    if shells:
        out_shape.append(jax.ShapeDtypeStruct(pool.shape, pool.dtype))
    return pl.pallas_call(
        functools.partial(conv_kernel, jobs=jobs, start=start, waits=len(after)),
        out_shape=out_shape,
        in_specs=[SMEM, SMEM, VMEM, VMEM, VMEM] + [ANY] * len(after) + [VMEM] * len(shells),
        out_specs=[VMEM] * len(out_shape),
        scratch_shapes=[
            pltpu.VMEM((3, BS + 2, pairs, 2 * BS, EXT), jnp.bfloat16),
            pltpu.VMEM((BS, BS, LANES), jnp.int32),
        ],
        input_output_aliases={4: 1} if shells else {},
        compiler_params=params(),
        cost_estimate=LITTLE,
        name="convolve_%d" % jobs[0][0],
    )(*tables, bias, bands, pool, *after, *shells)


def place_kernel(order_ref, *refs, distances):
    out_ref, sems = refs[-2:]
    names = [order_ref[r] for r in range(out_ref.shape[0])]

    def each(act):
        for distance, source in zip(distances, refs):
            items = source.shape[0]
            first = (lax.axis_index("gy") ^ distance) * items
            for r, name in enumerate(names):

                @pl.when((name >= first) & (name < first + items))
                def _():
                    act(pltpu.make_async_copy(source.at[name - first], out_ref.at[r], sems.at[r]))

    each(lambda copy: copy.start())
    each(lambda copy: copy.wait())


def placed(distances, receive_order, arrived, output):
    count = receive_order.shape[0]
    filled = () if output is None else (output,)
    return pl.pallas_call(
        functools.partial(place_kernel, distances=distances),
        out_shape=jax.ShapeDtypeStruct((count, ROWS, LANES), jnp.bfloat16),
        in_specs=[SMEM] + [ANY] * (len(distances) + len(filled)),
        out_specs=ANY,
        scratch_shapes=[pltpu.SemaphoreType.DMA((count,))],
        input_output_aliases={1 + len(distances): 0} if filled else {},
        compiler_params=params(),
        cost_estimate=LITTLE,
        name="place_%d" % distances[0],
    )(receive_order, *[arrived[m] for m in distances], *filled)


def exchanged(for_partner, for_other, axis):
    count = lax.axis_size(axis)
    others = [(i, i + 1) for i in range(1, count - 1, 2)]
    from_other = lax.ppermute(for_other, axis, others + [(j, i) for i, j in others])
    from_partner = lax.ppermute(for_partner, axis, [(i, i ^ 1) for i in range(count)])
    return from_partner, from_other


def on_device(
    features,
    occupancy,
    neighbors,
    face_lists,
    face_relays,
    send_slots,
    receive_order,
    weights,
    channel_bias,
):
    slots = features.shape[2]
    blocks = features.reshape(slots, ROWS, LANES)
    words = jnp.transpose(occupancy[0], (2, 0, 1))
    peers = send_slots.shape[2]
    faces = face_lists.shape[-1]
    rules = jnp.concatenate([words, jnp.transpose(neighbors[0], (2, 0, 1))], axis=0)
    tables = (jnp.transpose(send_slots[0, 0]), rules)
    bias = jnp.tile(channel_bias, GROUP).reshape(1, N_BAND)

    for_partner, for_other = masked_outgoing(face_lists, words, blocks, "gy")
    own_partner, own_other = masked_outgoing(face_relays, words, blocks, "gx", (for_partner,))
    y_partner, y_other = exchanged(for_partner, for_other, "gy")
    relay_partner, relay_other = relayed(face_relays, y_partner, y_other, own_partner, own_other, slots)
    x_partner, x_other = exchanged(relay_partner, relay_other, "gx")
    pool = masked_all(words, blocks, y_partner, y_other, slots + 2 * faces + 1, relay_partner)
    bands = banded(weights, relay_partner)

    far, near = list(range(peers // 2, peers)), list(reversed(range(1, peers // 2)))
    order = far + near + [0]
    arrived, shells, last = {}, (x_partner, x_other), ()
    for i, m in enumerate(order):
        first = i - (len(order) - 2)
        after = last + ((arrived[order[first]],) if 0 <= first < i else ())
        jobs = [(m, item) for item in range(send_slots.shape[3])]
        made = convolved(jobs, tables, bias, bands, pool, after, shells, slots + faces if shells else None)
        last = (made[0],)
        if shells:
            pool, shells = made[1], ()
        arrived[m] = lax.ppermute(made[0], "gy", [(d, d ^ m) for d in range(peers)]) if m else made[0]
    output = placed((0,) + tuple(far[:2]), receive_order[0, 0], arrived, None)
    if far[2:-1]:
        output = placed(tuple(far[2:-1]), receive_order[0, 0], arrived, output)
    output = placed(tuple(m for m in far[2:][-1:] + near), receive_order[0, 0], arrived, output)
    return output.reshape(1, 1, output.shape[0], BS, BS, LANES)


def solution(mesh):
    in_specs = (
        P("gx", "gy", None, None, None, None),
        P("gx", "gy", None, None),
        P("gx", "gy", None, None),
        P("gx", "gy", None),
        P("gx", "gy", None),
        P("gx", "gy", None, None),
        P("gx", "gy", None),
        P(),
        P(),
    )
    out_specs = P("gx", "gy", None, None, None, None)
    return jax.shard_map(
        on_device, mesh=mesh, in_specs=in_specs, out_specs=out_specs, check_vma=False
    )
```

```python
import functools

import jax
import jax.numpy as jnp
from jax import lax
from jax.experimental import pallas as pl
from jax.experimental.pallas import tpu as pltpu
from jax.sharding import PartitionSpec as P

C = 64
BS = 8
ROWS = BS * BS
LANES = BS * C
WORD_BITS = 21
GROUP = 4
K_BAND = (GROUP + 2) * C
N_BAND = GROUP * C
EXT = (BS + 2) * C
SHELL = (2 * BS, LANES + 6 * 128)
VMEM_LIMIT = 16 * 1024 * 1024
FIRST_LIMIT = 56 * 1024 * 1024

LITTLE = pl.CostEstimate(flops=1, bytes_accessed=1, transcendentals=0)

ANY = pl.BlockSpec(memory_space=pl.ANY)
HBM = pl.BlockSpec(memory_space=pltpu.HBM)
SMEM = pl.BlockSpec(memory_space=pltpu.SMEM)
VMEM = pl.BlockSpec(memory_space=pltpu.VMEM)


def params():
    return pltpu.CompilerParams(vmem_limit_bytes=VMEM_LIMIT)


def voxel_ids(x):
    rows = lax.broadcasted_iota(jnp.int32, (BS, LANES), 0)
    lanes = lax.broadcasted_iota(jnp.int32, (BS, LANES), 1)
    return x * ROWS + rows * BS + lanes // C


def shift_amounts(x):
    v = voxel_ids(x)
    first = (x * ROWS) // WORD_BITS
    last = (x * ROWS + ROWS - 1) // WORD_BITS
    amounts = v - first * WORD_BITS
    for k in range(first + 1, last + 1):
        amounts = jnp.where(v >= k * WORD_BITS, v - k * WORD_BITS, amounts)
    return amounts


def plane_bits(occ_ref, slot, x, shifts):
    v = voxel_ids(x)
    first = (x * ROWS) // WORD_BITS
    last = (x * ROWS + ROWS - 1) // WORD_BITS
    words = jnp.full((BS, LANES), occ_ref[first, 0, slot], jnp.int32)
    for k in range(first + 1, last + 1):
        words = jnp.where(v >= k * WORD_BITS, occ_ref[k, 0, slot], words)
    return lax.shift_right_logical(words, shifts) & 1


def masked_planes(occ_ref, slot, shift_ref, source):
    planes = []
    for i in range(BS // 2):
        values = source[pl.ds(2 * BS * i, 2 * BS), :].astype(jnp.float32)
        for half in range(2):
            x = 2 * i + half
            bits = plane_bits(occ_ref, slot, x, shift_ref[x])
            planes.append(jnp.where(bits > 0, values[half * BS : half * BS + BS], 0.0))
    return planes


def store_pair(ref, lanes, first, second):
    ref[:, lanes] = jnp.concatenate([first, second], axis=0).astype(jnp.bfloat16)


def store_block(ref, planes):
    for i in range(BS // 2):
        rows = pl.ds(2 * BS * i, 2 * BS)
        ref[rows, :] = jnp.concatenate(planes[2 * i : 2 * i + 2], axis=0).astype(jnp.bfloat16)


def columns_of(plane):
    return [plane[:, 128 * i : 128 * i + 128] for i in range(LANES // 128)]


def tile_ids():
    rows = lax.broadcasted_iota(jnp.int32, (BS, 128), 0)
    lanes = lax.broadcasted_iota(jnp.int32, (BS, 128), 1)
    return rows, lanes


def pack_shell(ref, planes):
    rows, lanes = tile_ids()
    store_pair(ref, pl.ds(0, LANES), planes[0], planes[BS - 1])
    edges, ends = [], []
    for x in range(1, BS - 1):
        columns = columns_of(planes[x])
        edges.append(jnp.where(lanes < C, columns[0], columns[-1]))
        end = columns[0]
        for i, column in enumerate(columns):
            if i:
                end = jnp.where(rows == i, pltpu.roll(column, i, 0), end)
            end = jnp.where(rows == 4 + i, pltpu.roll(column, (i + 5) % BS, 0), end)
        ends.append(end)
    for k in range(3):
        store_pair(ref, pl.ds(LANES + 128 * k, 128), edges[2 * k], edges[2 * k + 1])
        store_pair(ref, pl.ds(LANES + 128 * (3 + k), 128), ends[2 * k], ends[2 * k + 1])


def unpack_shell(ref, packed):
    rows, _ = tile_ids()
    outer = packed[:, pl.ds(0, LANES)].astype(jnp.float32)
    planes = [None] * BS
    planes[0], planes[BS - 1] = outer[:BS], outer[BS:]
    for k in range(3):
        edges = packed[:, pl.ds(LANES + 128 * k, 128)].astype(jnp.float32)
        ends = packed[:, pl.ds(LANES + 128 * (3 + k), 128)].astype(jnp.float32)
        for half in range(2):
            cut = slice(half * BS, half * BS + BS)
            edge, end = edges[cut], ends[cut]
            columns = []
            for i in range(4):
                first = pltpu.roll(end, (BS - i) % BS, 0) if i else end
                last = pltpu.roll(end, (3 - i) % BS, 0) if i != 3 else end
                columns.append(jnp.where(rows == 0, first, jnp.where(rows == BS - 1, last, edge)))
            planes[2 * k + 1 + half] = jnp.concatenate(columns, axis=1)
    store_block(ref, planes)


def upper_first(axis):
    return lax.axis_index(axis) % 2 == 0


def partner_offset(axis, width):
    return jnp.where(upper_first(axis), width, 0)


def outgoing_kernel(lists_ref, words_ref, feat_ref, *refs, axis):
    partner_ref, other_ref, held, shift_ref, lists, words, list_sems, sems = refs[-8:]
    slots = feat_ref.shape[0]
    width = partner_ref.shape[0]
    lists_in = pltpu.make_async_copy(lists_ref, lists, list_sems.at[0])
    words_in = pltpu.make_async_copy(words_ref, words, list_sems.at[1])
    lists_in.start()
    words_in.start()
    lists_in.wait()
    offset = partner_offset(axis, width)
    jobs = []
    for target, start in ((partner_ref, offset), (other_ref, width - offset)):
        for t in range(width):
            name = lists[0, 0, start + t]
            k = len(jobs)
            copy_in = pltpu.make_async_copy(feat_ref.at[jnp.minimum(name, slots - 1)], held.at[k], sems.at[k])
            copy_in.start()
            jobs.append((copy_in, name, target.at[t]))
    for x in range(BS):
        shift_ref[x] = shift_amounts(x)
    words_in.wait()
    for k, (copy_in, name, target) in enumerate(jobs):
        copy_in.wait()

        @pl.when(name < slots)
        def _():
            pack_shell(target, masked_planes(words, name, shift_ref, held.at[k]))


def masked_outgoing(lists, occupancy, features, axis, after=()):
    count = lists.shape[-1]
    half = jax.ShapeDtypeStruct((count // 2,) + SHELL, jnp.bfloat16)
    return pl.pallas_call(
        functools.partial(outgoing_kernel, axis=axis),
        out_shape=(half, half),
        in_specs=[HBM, HBM, HBM] + [ANY] * len(after),
        out_specs=(VMEM, VMEM),
        scratch_shapes=[
            pltpu.VMEM((count, ROWS, LANES), jnp.bfloat16),
            pltpu.VMEM((BS, BS, LANES), jnp.int32),
            pltpu.SMEM(lists.shape, jnp.int32),
            pltpu.SMEM(occupancy.shape, jnp.int32),
            pltpu.SemaphoreType.DMA((2,)),
            pltpu.SemaphoreType.DMA((count,)),
        ],
        compiler_params=pltpu.CompilerParams(vmem_limit_bytes=FIRST_LIMIT),
        cost_estimate=pl.CostEstimate(flops=2000000, bytes_accessed=2 * count * ROWS * LANES * 2, transcendentals=0),
        name="mask_outgoing_" + axis,
    )(lists, occupancy, features, *after)


def unpack_neighbors(pool_ref, start, axis, partner_ref, other_ref):
    width = partner_ref.shape[0]
    offset = partner_offset(axis, width)
    for t in range(width):
        unpack_shell(pool_ref.at[start + offset + t], partner_ref.at[t])
        unpack_shell(pool_ref.at[start + width - offset + t], other_ref.at[t])


def mask_all_kernel(occ_ref, feat_ref, partner_ref, other_ref, earlier_ref, pool_ref, shift_ref):
    slots = feat_ref.shape[0]
    for x in range(BS):
        shift_ref[x] = shift_amounts(x)
    pool_ref[pool_ref.shape[0] - 1] = jnp.zeros((ROWS, LANES), jnp.bfloat16)

    def body(t, carry):
        store_block(pool_ref.at[t], masked_planes(occ_ref, t, shift_ref, feat_ref.at[t]))
        return carry

    lax.fori_loop(0, slots, body, 0)
    unpack_neighbors(pool_ref, slots, "gy", partner_ref, other_ref)


def masked_all(occupancy, features, partner, other, pool_blocks, earlier):
    slots = features.shape[0]
    return pl.pallas_call(
        mask_all_kernel,
        out_shape=jax.ShapeDtypeStruct((pool_blocks, ROWS, LANES), jnp.bfloat16),
        in_specs=[SMEM, VMEM, VMEM, VMEM, ANY],
        out_specs=VMEM,
        scratch_shapes=[pltpu.VMEM((BS, BS, LANES), jnp.int32)],
        compiler_params=params(),
        cost_estimate=pl.CostEstimate(flops=8000000, bytes_accessed=3 * slots * ROWS * LANES * 2, transcendentals=0),
        name="mask_held",
    )(occupancy, features, partner, other, earlier)


def bands_kernel(weights_ref, earlier_ref, out_ref):
    zeros = jnp.zeros((C, C), jnp.float32)
    for pair in range(9):
        taps = [weights_ref[3 * pair + c].astype(jnp.float32) for c in range(3)]
        for z_in in range(GROUP + 2):
            row = [taps[z_in - z_out] if 0 <= z_in - z_out <= 2 else zeros for z_out in range(GROUP)]
            out_ref[pair, pl.ds(z_in * C, C), :] = jnp.concatenate(row, axis=1).astype(jnp.bfloat16)


def banded(weights, earlier):
    return pl.pallas_call(
        bands_kernel,
        out_shape=jax.ShapeDtypeStruct((9, K_BAND, N_BAND), jnp.bfloat16),
        in_specs=[VMEM, ANY],
        out_specs=VMEM,
        compiler_params=params(),
        cost_estimate=pl.CostEstimate(flops=100000, bytes_accessed=4000000, transcendentals=0),
        name="band_weights",
    )(weights, earlier)


def relay_kernel(relays_ref, partner_ref, other_ref, own_partner, own_other, out_partner, out_other, sems, *, slots):
    width = partner_ref.shape[0]
    offset = partner_offset("gx", width)

    def each(act):
        for part, (start, out) in enumerate(((offset, out_partner), (width - offset, out_other))):
            for t in range(width):
                index = relays_ref[0, 0, start + t] - slots
                from_partner = (index >= width) == upper_first("gy")
                place = index % width
                sem = sems.at[part * width + t]

                @pl.when((index >= 0) & from_partner)
                def _():
                    act(pltpu.make_async_copy(partner_ref.at[place], out.at[t], sem))

                @pl.when((index >= 0) & jnp.logical_not(from_partner))
                def _():
                    act(pltpu.make_async_copy(other_ref.at[place], out.at[t], sem))

    each(lambda copy: copy.start())
    each(lambda copy: copy.wait())


def relayed(face_relays, partner, other, own_partner, own_other, slots):
    half = jax.ShapeDtypeStruct(partner.shape, jnp.bfloat16)
    count = face_relays.shape[-1]
    return pl.pallas_call(
        functools.partial(relay_kernel, slots=slots),
        out_shape=(half, half),
        in_specs=[SMEM, ANY, ANY, ANY, ANY],
        out_specs=(ANY, ANY),
        scratch_shapes=[pltpu.SemaphoreType.DMA((count,))],
        input_output_aliases={3: 0, 4: 1},
        compiler_params=params(),
        cost_estimate=pl.CostEstimate(flops=0, bytes_accessed=2 * count * SHELL[0] * SHELL[1] * 2, transcendentals=0),
        name="gather_relays",
    )(face_relays, partner, other, own_partner, own_other)


def extended_plane(blocks, lane_low):
    below, own, above = blocks
    columns = [below] + [own[:, 128 * i : 128 * i + 128] for i in range(4)] + [above]
    turned = [pltpu.roll(column, C, 1) for column in columns]
    return [jnp.where(lane_low, turned[i], turned[i + 1]) for i in range(5)]


def conv_kernel(sent_in, table_in, bias_ref, bands_ref, pool_ref, *refs, jobs, start, waits):
    refs = list(refs)
    sems, table_ref, sent_ref, shift_ref, tiles = (refs.pop() for _ in range(5))
    copies = [
        pltpu.make_async_copy(source, target, sems.at[i])
        for i, (source, target) in enumerate(((sent_in, sent_ref), (table_in, table_ref)))
    ]
    for copy in copies:
        copy.start()
    del refs[:waits]
    if start is None:
        pool = pool_ref
    else:
        pool = refs.pop()
        unpack_neighbors(pool, start, "gx", refs.pop(0), refs.pop(0))
    (out_ref,) = refs
    items = len(jobs)
    pairs = (items + 1) // 2
    for x in range(BS):
        shift_ref[x] = shift_amounts(x)
    for copy in copies:
        copy.wait()
    me = lax.axis_index("gy")
    offsets = table_ref.shape[0] - 27
    slots = [jnp.maximum(sent_ref[item, me ^ distance], 0) for distance, item in jobs]
    slots = slots + slots[-1:] * (2 * pairs - items)

    row_ids = lax.broadcasted_iota(jnp.int32, (BS, 128), 0)
    lane_low = lax.broadcasted_iota(jnp.int32, (2 * BS, 128), 1) < C
    is_last = row_ids == BS - 1
    is_first = row_ids == 0

    def row_pair(slot, depth_x, depth_y, i):
        row = offsets + 9 * depth_x + 3 * depth_y
        rows = pl.ds(2 * BS * i, 2 * BS)
        below = pool[table_ref[row, 0, slot], rows, pl.ds(LANES - 128, 128)]
        own = pool[table_ref[row + 1, 0, slot], rows, :]
        above = pool[table_ref[row + 2, 0, slot], rows, pl.ds(0, 128)]
        return extended_plane([v.astype(jnp.float32) for v in (below, own, above)], lane_low)

    def build(pair, both):
        for depth_x, i in ((0, 3), (1, 0), (1, 1), (1, 2), (1, 3), (2, 0)):
            rows = [[row_pair(slot, depth_x, depth_y, i) for depth_y in range(3)] for slot in both]
            if depth_x == 0:
                planes = ((1, 0),)
            elif depth_x == 2:
                planes = ((0, BS + 1),)
            else:
                planes = ((0, 2 * i + 1), (1, 2 * i + 2))
            for half, plane in planes:
                cut = slice(half * BS, half * BS + BS)
                for column in range(5):
                    lanes = pl.ds(128 * column, 128)
                    shifted = ([], [], [])
                    for k in range(2):
                        before, own, after = (rows[k][depth_y][column][cut] for depth_y in range(3))
                        shifted[0].append(pltpu.roll(jnp.where(is_last, before, own), 1, 0))
                        shifted[1].append(own)
                        shifted[2].append(pltpu.roll(jnp.where(is_first, after, own), BS - 1, 0))
                    for depth_y in range(3):
                        tiles[depth_y, plane, pair, :, lanes] = jnp.concatenate(shifted[depth_y], axis=0).astype(
                            jnp.bfloat16
                        )

    for pair in range(pairs):
        build(pair, slots[2 * pair : 2 * pair + 2])

    bias = bias_ref[...]
    for group in range(BS // GROUP):
        window = pl.ds(group * N_BAND, K_BAND)
        windows = [
            tiles[depth_y, pl.ds(depth_x, BS), :, :, window].reshape(BS * pairs * 2 * BS, K_BAND)
            for depth_x in range(3)
            for depth_y in range(3)
        ]
        total = jnp.dot(
            jnp.concatenate(windows, axis=1),
            bands_ref[...].reshape(9 * K_BAND, N_BAND),
            preferred_element_type=jnp.float32,
        )
        total = (total + bias).reshape(BS, pairs * 2, BS, N_BAND)
        for item in range(items):
            slot = slots[item]
            for i in range(BS // 2):
                parts = []
                for x in (2 * i, 2 * i + 1):
                    bits = plane_bits(table_ref, slot, x, shift_ref[x])[:, group * N_BAND : group * N_BAND + N_BAND]
                    parts.append(jnp.where(bits > 0, total[x, item], 0.0))
                out_ref[item, pl.ds(2 * BS * i, 2 * BS), pl.ds(group * N_BAND, N_BAND)] = jnp.concatenate(
                    parts, axis=0
                ).astype(jnp.bfloat16)


def convolved(jobs, tables, bias, bands, pool, after, shells=(), start=None):
    pairs = (len(jobs) + 1) // 2
    out_shape = [jax.ShapeDtypeStruct((len(jobs), ROWS, LANES), jnp.bfloat16)]
    if shells:
        out_shape.append(jax.ShapeDtypeStruct(pool.shape, pool.dtype))
    return pl.pallas_call(
        functools.partial(conv_kernel, jobs=jobs, start=start, waits=len(after)),
        out_shape=out_shape,
        in_specs=[ANY, ANY, VMEM, VMEM, VMEM] + [ANY] * len(after) + [VMEM] * len(shells),
        out_specs=[VMEM] * len(out_shape),
        scratch_shapes=[
            pltpu.VMEM((3, BS + 2, pairs, 2 * BS, EXT), jnp.bfloat16),
            pltpu.VMEM((BS, BS, LANES), jnp.int32),
            pltpu.SMEM(tables[0].shape, jnp.int32),
            pltpu.SMEM(tables[1].shape, jnp.int32),
            pltpu.SemaphoreType.DMA((2,)),
        ],
        input_output_aliases={4: 1} if shells else {},
        compiler_params=params(),
        cost_estimate=LITTLE,
        name="convolve_%d" % jobs[0][0],
    )(*tables, bias, bands, pool, *after, *shells)


def place_kernel(order_ref, *refs, distances):
    out_ref, sems = refs[-2:]
    names = [order_ref[r] for r in range(out_ref.shape[0])]

    def each(act):
        for distance, source in zip(distances, refs):
            items = source.shape[0]
            first = (lax.axis_index("gy") ^ distance) * items
            for r, name in enumerate(names):

                @pl.when((name >= first) & (name < first + items))
                def _():
                    act(pltpu.make_async_copy(source.at[name - first], out_ref.at[r], sems.at[r]))

    each(lambda copy: copy.start())
    each(lambda copy: copy.wait())


def placed(distances, receive_order, arrived, output):
    count = receive_order.shape[0]
    filled = () if output is None else (output,)
    return pl.pallas_call(
        functools.partial(place_kernel, distances=distances),
        out_shape=jax.ShapeDtypeStruct((count, ROWS, LANES), jnp.bfloat16),
        in_specs=[SMEM] + [ANY] * (len(distances) + len(filled)),
        out_specs=ANY,
        scratch_shapes=[pltpu.SemaphoreType.DMA((count,))],
        input_output_aliases={1 + len(distances): 0} if filled else {},
        compiler_params=params(),
        cost_estimate=LITTLE,
        name="place_%d" % distances[0],
    )(receive_order, *[arrived[m] for m in distances], *filled)


def exchanged(for_partner, for_other, axis):
    count = lax.axis_size(axis)
    others = [(i, i + 1) for i in range(1, count - 1, 2)]
    from_other = lax.ppermute(for_other, axis, others + [(j, i) for i, j in others])
    from_partner = lax.ppermute(for_partner, axis, [(i, i ^ 1) for i in range(count)])
    return from_partner, from_other


def on_device(
    features,
    occupancy,
    neighbors,
    face_lists,
    face_relays,
    send_slots,
    receive_order,
    weights,
    channel_bias,
):
    slots = features.shape[2]
    blocks = features.reshape(slots, ROWS, LANES)
    words = jnp.transpose(occupancy[0], (2, 0, 1))
    peers = send_slots.shape[2]
    faces = face_lists.shape[-1]
    rules = jnp.concatenate([words, jnp.transpose(neighbors[0], (2, 0, 1))], axis=0)
    tables = (jnp.transpose(send_slots[0, 0]), rules)
    bias = jnp.tile(channel_bias, GROUP).reshape(1, N_BAND)

    for_partner, for_other = masked_outgoing(face_lists, words, blocks, "gy")
    own_partner, own_other = masked_outgoing(face_relays, words, blocks, "gx", (for_partner,))
    y_partner, y_other = exchanged(for_partner, for_other, "gy")
    relay_partner, relay_other = relayed(face_relays, y_partner, y_other, own_partner, own_other, slots)
    x_partner, x_other = exchanged(relay_partner, relay_other, "gx")
    pool = masked_all(words, blocks, y_partner, y_other, slots + 2 * faces + 1, relay_partner)
    bands = banded(weights, relay_partner)

    far, near = list(range(peers // 2, peers)), list(reversed(range(1, peers // 2)))
    order = far + near + [0]
    arrived, shells, last = {}, (x_partner, x_other), ()
    for i, m in enumerate(order):
        first = i - (len(order) - 2)
        after = last + ((arrived[order[first]],) if 0 <= first < i else ())
        jobs = [(m, item) for item in range(send_slots.shape[3])]
        made = convolved(jobs, tables, bias, bands, pool, after, shells, slots + faces if shells else None)
        last = (made[0],)
        if shells:
            pool, shells = made[1], ()
        arrived[m] = lax.ppermute(made[0], "gy", [(d, d ^ m) for d in range(peers)]) if m else made[0]
    output = placed((0,) + tuple(far[:2]), receive_order[0, 0], arrived, None)
    if far[2:-1]:
        output = placed(tuple(far[2:-1]), receive_order[0, 0], arrived, output)
    output = placed(tuple(m for m in far[2:][-1:] + near), receive_order[0, 0], arrived, output)
    return output.reshape(1, 1, output.shape[0], BS, BS, LANES)


def solution(mesh):
    in_specs = (
        P("gx", "gy", None, None, None, None),
        P("gx", "gy", None, None),
        P("gx", "gy", None, None),
        P("gx", "gy", None),
        P("gx", "gy", None),
        P("gx", "gy", None, None),
        P("gx", "gy", None),
        P(),
        P(),
    )
    out_specs = P("gx", "gy", None, None, None, None)
    return jax.shard_map(
        on_device, mesh=mesh, in_specs=in_specs, out_specs=out_specs, check_vma=False
    )
```

```python
import functools

import jax
import jax.numpy as jnp
from jax import lax
from jax.experimental import pallas as pl
from jax.experimental.pallas import tpu as pltpu
from jax.sharding import PartitionSpec as P

C = 64
BS = 8
ROWS = BS * BS
LANES = BS * C
WORD_BITS = 21
GROUP = 4
K_BAND = (GROUP + 2) * C
N_BAND = GROUP * C
EXT = (BS + 2) * C
SHELL = (2 * BS, LANES + 6 * 128)
VMEM_LIMIT = 16 * 1024 * 1024
FIRST_LIMIT = 56 * 1024 * 1024

LITTLE = pl.CostEstimate(flops=1, bytes_accessed=1, transcendentals=0)

ANY = pl.BlockSpec(memory_space=pl.ANY)
HBM = pl.BlockSpec(memory_space=pltpu.HBM)
SMEM = pl.BlockSpec(memory_space=pltpu.SMEM)
VMEM = pl.BlockSpec(memory_space=pltpu.VMEM)


def params():
    return pltpu.CompilerParams(vmem_limit_bytes=VMEM_LIMIT)


def voxel_ids(x):
    rows = lax.broadcasted_iota(jnp.int32, (BS, LANES), 0)
    lanes = lax.broadcasted_iota(jnp.int32, (BS, LANES), 1)
    return x * ROWS + rows * BS + lanes // C


def shift_amounts(x):
    v = voxel_ids(x)
    first = (x * ROWS) // WORD_BITS
    last = (x * ROWS + ROWS - 1) // WORD_BITS
    amounts = v - first * WORD_BITS
    for k in range(first + 1, last + 1):
        amounts = jnp.where(v >= k * WORD_BITS, v - k * WORD_BITS, amounts)
    return amounts


def plane_bits(occ_ref, slot, x, shifts):
    v = voxel_ids(x)
    first = (x * ROWS) // WORD_BITS
    last = (x * ROWS + ROWS - 1) // WORD_BITS
    words = jnp.full((BS, LANES), occ_ref[first, 0, slot], jnp.int32)
    for k in range(first + 1, last + 1):
        words = jnp.where(v >= k * WORD_BITS, occ_ref[k, 0, slot], words)
    return lax.shift_right_logical(words, shifts) & 1


def masked_planes(occ_ref, slot, shift_ref, source):
    planes = []
    for i in range(BS // 2):
        values = source[pl.ds(2 * BS * i, 2 * BS), :].astype(jnp.float32)
        for half in range(2):
            x = 2 * i + half
            bits = plane_bits(occ_ref, slot, x, shift_ref[x])
            planes.append(jnp.where(bits > 0, values[half * BS : half * BS + BS], 0.0))
    return planes


def store_pair(ref, lanes, first, second):
    ref[:, lanes] = jnp.concatenate([first, second], axis=0).astype(jnp.bfloat16)


def store_block(ref, planes):
    for i in range(BS // 2):
        rows = pl.ds(2 * BS * i, 2 * BS)
        ref[rows, :] = jnp.concatenate(planes[2 * i : 2 * i + 2], axis=0).astype(jnp.bfloat16)


def columns_of(plane):
    return [plane[:, 128 * i : 128 * i + 128] for i in range(LANES // 128)]


def tile_ids():
    rows = lax.broadcasted_iota(jnp.int32, (BS, 128), 0)
    lanes = lax.broadcasted_iota(jnp.int32, (BS, 128), 1)
    return rows, lanes


def pack_shell(ref, planes):
    rows, lanes = tile_ids()
    store_pair(ref, pl.ds(0, LANES), planes[0], planes[BS - 1])
    edges, ends = [], []
    for x in range(1, BS - 1):
        columns = columns_of(planes[x])
        edges.append(jnp.where(lanes < C, columns[0], columns[-1]))
        end = columns[0]
        for i, column in enumerate(columns):
            if i:
                end = jnp.where(rows == i, pltpu.roll(column, i, 0), end)
            end = jnp.where(rows == 4 + i, pltpu.roll(column, (i + 5) % BS, 0), end)
        ends.append(end)
    for k in range(3):
        store_pair(ref, pl.ds(LANES + 128 * k, 128), edges[2 * k], edges[2 * k + 1])
        store_pair(ref, pl.ds(LANES + 128 * (3 + k), 128), ends[2 * k], ends[2 * k + 1])


def unpack_shell(ref, packed):
    rows, _ = tile_ids()
    outer = packed[:, pl.ds(0, LANES)].astype(jnp.float32)
    planes = [None] * BS
    planes[0], planes[BS - 1] = outer[:BS], outer[BS:]
    for k in range(3):
        edges = packed[:, pl.ds(LANES + 128 * k, 128)].astype(jnp.float32)
        ends = packed[:, pl.ds(LANES + 128 * (3 + k), 128)].astype(jnp.float32)
        for half in range(2):
            cut = slice(half * BS, half * BS + BS)
            edge, end = edges[cut], ends[cut]
            columns = []
            for i in range(4):
                first = pltpu.roll(end, (BS - i) % BS, 0) if i else end
                last = pltpu.roll(end, (3 - i) % BS, 0) if i != 3 else end
                columns.append(jnp.where(rows == 0, first, jnp.where(rows == BS - 1, last, edge)))
            planes[2 * k + 1 + half] = jnp.concatenate(columns, axis=1)
    store_block(ref, planes)


def upper_first(axis):
    return lax.axis_index(axis) % 2 == 0


def partner_offset(axis, width):
    return jnp.where(upper_first(axis), width, 0)


def outgoing_kernel(lists_ref, words_ref, feat_ref, *refs, axis):
    partner_ref, other_ref, held, shift_ref, lists, words, list_sems, sems = refs[-8:]
    slots = feat_ref.shape[0]
    width = partner_ref.shape[0]
    lists_in = pltpu.make_async_copy(lists_ref, lists, list_sems.at[0])
    words_in = pltpu.make_async_copy(words_ref, words, list_sems.at[1])
    lists_in.start()
    words_in.start()
    lists_in.wait()
    offset = partner_offset(axis, width)
    jobs = []
    for target, start in ((partner_ref, offset), (other_ref, width - offset)):
        for t in range(width):
            name = lists[0, 0, start + t]
            k = len(jobs)
            copy_in = pltpu.make_async_copy(feat_ref.at[jnp.minimum(name, slots - 1)], held.at[k], sems.at[k])
            copy_in.start()
            jobs.append((copy_in, name, target.at[t]))
    for x in range(BS):
        shift_ref[x] = shift_amounts(x)
    words_in.wait()
    for k, (copy_in, name, target) in enumerate(jobs):
        copy_in.wait()

        @pl.when(name < slots)
        def _():
            pack_shell(target, masked_planes(words, name, shift_ref, held.at[k]))


def masked_outgoing(lists, occupancy, features, axis, after=()):
    count = lists.shape[-1]
    half = jax.ShapeDtypeStruct((count // 2,) + SHELL, jnp.bfloat16)
    return pl.pallas_call(
        functools.partial(outgoing_kernel, axis=axis),
        out_shape=(half, half),
        in_specs=[HBM, HBM, HBM] + [ANY] * len(after),
        out_specs=(VMEM, VMEM),
        scratch_shapes=[
            pltpu.VMEM((count, ROWS, LANES), jnp.bfloat16),
            pltpu.VMEM((BS, BS, LANES), jnp.int32),
            pltpu.SMEM(lists.shape, jnp.int32),
            pltpu.SMEM(occupancy.shape, jnp.int32),
            pltpu.SemaphoreType.DMA((2,)),
            pltpu.SemaphoreType.DMA((count,)),
        ],
        compiler_params=pltpu.CompilerParams(vmem_limit_bytes=FIRST_LIMIT),
        cost_estimate=pl.CostEstimate(flops=2000000, bytes_accessed=2 * count * ROWS * LANES * 2, transcendentals=0),
        name="mask_outgoing_" + axis,
    )(lists, occupancy, features, *after)


def unpack_neighbors(pool_ref, start, axis, partner_ref, other_ref):
    width = partner_ref.shape[0]
    offset = partner_offset(axis, width)
    for t in range(width):
        unpack_shell(pool_ref.at[start + offset + t], partner_ref.at[t])
        unpack_shell(pool_ref.at[start + width - offset + t], other_ref.at[t])


def mask_all_kernel(occ_ref, feat_ref, partner_ref, other_ref, earlier_ref, pool_ref, shift_ref):
    slots = feat_ref.shape[0]
    for x in range(BS):
        shift_ref[x] = shift_amounts(x)
    pool_ref[pool_ref.shape[0] - 1] = jnp.zeros((ROWS, LANES), jnp.bfloat16)

    def body(t, carry):
        store_block(pool_ref.at[t], masked_planes(occ_ref, t, shift_ref, feat_ref.at[t]))
        return carry

    lax.fori_loop(0, slots, body, 0)
    unpack_neighbors(pool_ref, slots, "gy", partner_ref, other_ref)


def masked_all(occupancy, features, partner, other, pool_blocks, earlier):
    slots = features.shape[0]
    return pl.pallas_call(
        mask_all_kernel,
        out_shape=jax.ShapeDtypeStruct((pool_blocks, ROWS, LANES), jnp.bfloat16),
        in_specs=[SMEM, VMEM, VMEM, VMEM, ANY],
        out_specs=VMEM,
        scratch_shapes=[pltpu.VMEM((BS, BS, LANES), jnp.int32)],
        compiler_params=params(),
        cost_estimate=pl.CostEstimate(flops=8000000, bytes_accessed=3 * slots * ROWS * LANES * 2, transcendentals=0),
        name="mask_held",
    )(occupancy, features, partner, other, earlier)


def bands_kernel(weights_ref, earlier_ref, out_ref):
    zeros = jnp.zeros((C, C), jnp.float32)
    for pair in range(9):
        taps = [weights_ref[3 * pair + c].astype(jnp.float32) for c in range(3)]
        for z_in in range(GROUP + 2):
            row = [taps[z_in - z_out] if 0 <= z_in - z_out <= 2 else zeros for z_out in range(GROUP)]
            out_ref[pair, pl.ds(z_in * C, C), :] = jnp.concatenate(row, axis=1).astype(jnp.bfloat16)


def banded(weights, earlier):
    return pl.pallas_call(
        bands_kernel,
        out_shape=jax.ShapeDtypeStruct((9, K_BAND, N_BAND), jnp.bfloat16),
        in_specs=[VMEM, ANY],
        out_specs=VMEM,
        compiler_params=params(),
        cost_estimate=pl.CostEstimate(flops=100000, bytes_accessed=4000000, transcendentals=0),
        name="band_weights",
    )(weights, earlier)


def relay_kernel(relays_ref, partner_ref, other_ref, own_partner, own_other, out_partner, out_other, sems, *, slots):
    width = partner_ref.shape[0]
    offset = partner_offset("gx", width)

    def each(act):
        for part, (start, out) in enumerate(((offset, out_partner), (width - offset, out_other))):
            for t in range(width):
                index = relays_ref[0, 0, start + t] - slots
                from_partner = (index >= width) == upper_first("gy")
                place = index % width
                sem = sems.at[part * width + t]

                @pl.when((index >= 0) & from_partner)
                def _():
                    act(pltpu.make_async_copy(partner_ref.at[place], out.at[t], sem))

                @pl.when((index >= 0) & jnp.logical_not(from_partner))
                def _():
                    act(pltpu.make_async_copy(other_ref.at[place], out.at[t], sem))

    each(lambda copy: copy.start())
    each(lambda copy: copy.wait())


def relayed(face_relays, partner, other, own_partner, own_other, slots):
    half = jax.ShapeDtypeStruct(partner.shape, jnp.bfloat16)
    count = face_relays.shape[-1]
    return pl.pallas_call(
        functools.partial(relay_kernel, slots=slots),
        out_shape=(half, half),
        in_specs=[SMEM, ANY, ANY, ANY, ANY],
        out_specs=(ANY, ANY),
        scratch_shapes=[pltpu.SemaphoreType.DMA((count,))],
        input_output_aliases={3: 0, 4: 1},
        compiler_params=params(),
        cost_estimate=pl.CostEstimate(flops=0, bytes_accessed=2 * count * SHELL[0] * SHELL[1] * 2, transcendentals=0),
        name="gather_relays",
    )(face_relays, partner, other, own_partner, own_other)


def extended_plane(blocks, lane_low):
    below, own, above = blocks
    columns = [below] + [own[:, 128 * i : 128 * i + 128] for i in range(4)] + [above]
    turned = [pltpu.roll(column, C, 1) for column in columns]
    return [jnp.where(lane_low, turned[i], turned[i + 1]) for i in range(5)]


def conv_kernel(sent_in, table_in, bias_ref, bands_ref, pool_ref, *refs, jobs, start, waits):
    refs = list(refs)
    sems, table_ref, sent_ref, shift_ref, tiles = (refs.pop() for _ in range(5))
    copies = [
        pltpu.make_async_copy(source, target, sems.at[i])
        for i, (source, target) in enumerate(((sent_in, sent_ref), (table_in, table_ref)))
    ]
    for copy in copies:
        copy.start()
    del refs[:waits]
    if start is None:
        pool = pool_ref
    else:
        pool = refs.pop()
        unpack_neighbors(pool, start, "gx", refs.pop(0), refs.pop(0))
    (out_ref,) = refs
    items = len(jobs)
    pairs = (items + 1) // 2
    for x in range(BS):
        shift_ref[x] = shift_amounts(x)
    for copy in copies:
        copy.wait()
    me = lax.axis_index("gy")
    offsets = table_ref.shape[0] - 27
    slots = [jnp.maximum(sent_ref[item, me ^ distance], 0) for distance, item in jobs]
    slots = slots + slots[-1:] * (2 * pairs - items)

    row_ids = lax.broadcasted_iota(jnp.int32, (BS, 128), 0)
    lane_low = lax.broadcasted_iota(jnp.int32, (2 * BS, 128), 1) < C
    is_last = row_ids == BS - 1
    is_first = row_ids == 0

    def row_pair(slot, depth_x, depth_y, i):
        row = offsets + 9 * depth_x + 3 * depth_y
        rows = pl.ds(2 * BS * i, 2 * BS)
        below = pool[table_ref[row, 0, slot], rows, pl.ds(LANES - 128, 128)]
        own = pool[table_ref[row + 1, 0, slot], rows, :]
        above = pool[table_ref[row + 2, 0, slot], rows, pl.ds(0, 128)]
        return extended_plane([v.astype(jnp.float32) for v in (below, own, above)], lane_low)

    def build(pair, both):
        for depth_x, i in ((0, 3), (1, 0), (1, 1), (1, 2), (1, 3), (2, 0)):
            rows = [[row_pair(slot, depth_x, depth_y, i) for depth_y in range(3)] for slot in both]
            if depth_x == 0:
                planes = ((1, 0),)
            elif depth_x == 2:
                planes = ((0, BS + 1),)
            else:
                planes = ((0, 2 * i + 1), (1, 2 * i + 2))
            for half, plane in planes:
                cut = slice(half * BS, half * BS + BS)
                for column in range(5):
                    lanes = pl.ds(128 * column, 128)
                    shifted = ([], [], [])
                    for k in range(2):
                        before, own, after = (rows[k][depth_y][column][cut] for depth_y in range(3))
                        shifted[0].append(pltpu.roll(jnp.where(is_last, before, own), 1, 0))
                        shifted[1].append(own)
                        shifted[2].append(pltpu.roll(jnp.where(is_first, after, own), BS - 1, 0))
                    for depth_y in range(3):
                        tiles[depth_y, plane, pair, :, lanes] = jnp.concatenate(shifted[depth_y], axis=0).astype(
                            jnp.bfloat16
                        )

    for pair in range(pairs):
        build(pair, slots[2 * pair : 2 * pair + 2])

    bias = bias_ref[...]
    for group in range(BS // GROUP):
        window = pl.ds(group * N_BAND, K_BAND)
        windows = [
            tiles[depth_y, pl.ds(depth_x, BS), :, :, window].reshape(BS * pairs * 2 * BS, K_BAND)
            for depth_x in range(3)
            for depth_y in range(3)
        ]
        total = jnp.dot(
            jnp.concatenate(windows, axis=1),
            bands_ref[...].reshape(9 * K_BAND, N_BAND),
            preferred_element_type=jnp.float32,
        )
        total = (total + bias).reshape(BS, pairs * 2, BS, N_BAND)
        for item in range(items):
            slot = slots[item]
            for i in range(BS // 2):
                parts = []
                for x in (2 * i, 2 * i + 1):
                    bits = plane_bits(table_ref, slot, x, shift_ref[x])[:, group * N_BAND : group * N_BAND + N_BAND]
                    parts.append(jnp.where(bits > 0, total[x, item], 0.0))
                out_ref[item, pl.ds(2 * BS * i, 2 * BS), pl.ds(group * N_BAND, N_BAND)] = jnp.concatenate(
                    parts, axis=0
                ).astype(jnp.bfloat16)


def convolved(jobs, tables, bias, bands, pool, after, shells=(), start=None):
    pairs = (len(jobs) + 1) // 2
    out_shape = [jax.ShapeDtypeStruct((len(jobs), ROWS, LANES), jnp.bfloat16)]
    if shells:
        out_shape.append(jax.ShapeDtypeStruct(pool.shape, pool.dtype))
    return pl.pallas_call(
        functools.partial(conv_kernel, jobs=jobs, start=start, waits=len(after)),
        out_shape=out_shape,
        in_specs=[ANY, ANY, VMEM, VMEM, VMEM] + [ANY] * len(after) + [VMEM] * len(shells),
        out_specs=[VMEM] * len(out_shape),
        scratch_shapes=[
            pltpu.VMEM((3, BS + 2, pairs, 2 * BS, EXT), jnp.bfloat16),
            pltpu.VMEM((BS, BS, LANES), jnp.int32),
            pltpu.SMEM(tables[0].shape, jnp.int32),
            pltpu.SMEM(tables[1].shape, jnp.int32),
            pltpu.SemaphoreType.DMA((2,)),
        ],
        input_output_aliases={4: 1} if shells else {},
        compiler_params=params(),
        cost_estimate=LITTLE,
        name="convolve_%d" % jobs[0][0],
    )(*tables, bias, bands, pool, *after, *shells)


def place_kernel(order_ref, *refs, distances):
    out_ref, sems = refs[-2:]
    names = [order_ref[r] for r in range(out_ref.shape[0])]

    def each(act):
        for distance, source in zip(distances, refs):
            items = source.shape[0]
            first = (lax.axis_index("gy") ^ distance) * items
            for r, name in enumerate(names):

                @pl.when((name >= first) & (name < first + items))
                def _():
                    act(pltpu.make_async_copy(source.at[name - first], out_ref.at[r], sems.at[r]))

    each(lambda copy: copy.start())
    each(lambda copy: copy.wait())


def placed(distances, receive_order, arrived, output):
    count = receive_order.shape[0]
    filled = () if output is None else (output,)
    return pl.pallas_call(
        functools.partial(place_kernel, distances=distances),
        out_shape=jax.ShapeDtypeStruct((count, ROWS, LANES), jnp.bfloat16),
        in_specs=[SMEM] + [ANY] * (len(distances) + len(filled)),
        out_specs=ANY,
        scratch_shapes=[pltpu.SemaphoreType.DMA((count,))],
        input_output_aliases={1 + len(distances): 0} if filled else {},
        compiler_params=params(),
        cost_estimate=LITTLE,
        name="place_%d" % distances[0],
    )(receive_order, *[arrived[m] for m in distances], *filled)


def exchanged(for_partner, for_other, axis):
    count = lax.axis_size(axis)
    others = [(i, i + 1) for i in range(1, count - 1, 2)]
    from_other = lax.ppermute(for_other, axis, others + [(j, i) for i, j in others])
    from_partner = lax.ppermute(for_partner, axis, [(i, i ^ 1) for i in range(count)])
    return from_partner, from_other


def on_device(
    features,
    occupancy,
    neighbors,
    face_lists,
    face_relays,
    send_slots,
    receive_order,
    weights,
    channel_bias,
):
    slots = features.shape[2]
    blocks = features.reshape(slots, ROWS, LANES)
    words = jnp.transpose(occupancy[0], (2, 0, 1))
    peers = send_slots.shape[2]
    faces = face_lists.shape[-1]
    rules = jnp.concatenate([words, jnp.transpose(neighbors[0], (2, 0, 1))], axis=0)
    tables = (jnp.transpose(send_slots[0, 0]), rules)
    bias = jnp.tile(channel_bias, GROUP).reshape(1, N_BAND)

    for_partner, for_other = masked_outgoing(face_lists, words, blocks, "gy")
    own_partner, own_other = masked_outgoing(face_relays, words, blocks, "gx", (for_partner,))
    y_partner, y_other = exchanged(for_partner, for_other, "gy")
    relay_partner, relay_other = relayed(face_relays, y_partner, y_other, own_partner, own_other, slots)
    x_partner, x_other = exchanged(relay_partner, relay_other, "gx")
    pool = masked_all(words, blocks, y_partner, y_other, slots + 2 * faces + 1, relay_partner)
    bands = banded(weights, relay_partner)

    far = list(range(3 * peers // 4, peers)) + list(range(peers // 2, 3 * peers // 4))
    near = list(reversed(range(1, peers // 2)))
    order = far + near + [0]
    arrived, shells, last = {}, (x_partner, x_other), ()
    for i, m in enumerate(order):
        first = i - (len(order) - 2)
        after = last + ((arrived[order[first]],) if 0 <= first < i else ())
        jobs = [(m, item) for item in range(send_slots.shape[3])]
        made = convolved(jobs, tables, bias, bands, pool, after, shells, slots + faces if shells else None)
        last = (made[0],)
        if shells:
            pool, shells = made[1], ()
        arrived[m] = lax.ppermute(made[0], "gy", [(d, d ^ m) for d in range(peers)]) if m else made[0]
    output = placed((0,) + tuple(far[:2]), receive_order[0, 0], arrived, None)
    output = placed(tuple(far[2:-1] + near), receive_order[0, 0], arrived, output)
    output = placed(tuple(far[2:][-1:]), receive_order[0, 0], arrived, output)
    return output.reshape(1, 1, output.shape[0], BS, BS, LANES)


def solution(mesh):
    in_specs = (
        P("gx", "gy", None, None, None, None),
        P("gx", "gy", None, None),
        P("gx", "gy", None, None),
        P("gx", "gy", None),
        P("gx", "gy", None),
        P("gx", "gy", None, None),
        P("gx", "gy", None),
        P(),
        P(),
    )
    out_specs = P("gx", "gy", None, None, None, None)
    return jax.shard_map(
        on_device, mesh=mesh, in_specs=in_specs, out_specs=out_specs, check_vma=False
    )
```

```python
import functools

import jax
import jax.numpy as jnp
from jax import lax
from jax.experimental import pallas as pl
from jax.experimental.pallas import tpu as pltpu
from jax.sharding import PartitionSpec as P

C = 64
BS = 8
ROWS = BS * BS
LANES = BS * C
WORD_BITS = 21
GROUP = 4
K_BAND = (GROUP + 2) * C
N_BAND = GROUP * C
EXT = (BS + 2) * C
SHELL = (2 * BS, LANES + 6 * 128)
VMEM_LIMIT = 16 * 1024 * 1024
FIRST_LIMIT = 56 * 1024 * 1024

LITTLE = pl.CostEstimate(flops=1, bytes_accessed=1, transcendentals=0)

ANY = pl.BlockSpec(memory_space=pl.ANY)
HBM = pl.BlockSpec(memory_space=pltpu.HBM)
SMEM = pl.BlockSpec(memory_space=pltpu.SMEM)
VMEM = pl.BlockSpec(memory_space=pltpu.VMEM)


def params():
    return pltpu.CompilerParams(vmem_limit_bytes=VMEM_LIMIT)


def voxel_ids(x):
    rows = lax.broadcasted_iota(jnp.int32, (BS, LANES), 0)
    lanes = lax.broadcasted_iota(jnp.int32, (BS, LANES), 1)
    return x * ROWS + rows * BS + lanes // C


def shift_amounts(x):
    v = voxel_ids(x)
    first = (x * ROWS) // WORD_BITS
    last = (x * ROWS + ROWS - 1) // WORD_BITS
    amounts = v - first * WORD_BITS
    for k in range(first + 1, last + 1):
        amounts = jnp.where(v >= k * WORD_BITS, v - k * WORD_BITS, amounts)
    return amounts


def plane_bits(occ_ref, slot, x, shifts):
    v = voxel_ids(x)
    first = (x * ROWS) // WORD_BITS
    last = (x * ROWS + ROWS - 1) // WORD_BITS
    words = jnp.full((BS, LANES), occ_ref[first, 0, slot], jnp.int32)
    for k in range(first + 1, last + 1):
        words = jnp.where(v >= k * WORD_BITS, occ_ref[k, 0, slot], words)
    return lax.shift_right_logical(words, shifts) & 1


def masked_planes(occ_ref, slot, shift_ref, source):
    planes = []
    for i in range(BS // 2):
        values = source[pl.ds(2 * BS * i, 2 * BS), :].astype(jnp.float32)
        for half in range(2):
            x = 2 * i + half
            bits = plane_bits(occ_ref, slot, x, shift_ref[x])
            planes.append(jnp.where(bits > 0, values[half * BS : half * BS + BS], 0.0))
    return planes


def store_pair(ref, lanes, first, second):
    ref[:, lanes] = jnp.concatenate([first, second], axis=0).astype(jnp.bfloat16)


def store_block(ref, planes):
    for i in range(BS // 2):
        rows = pl.ds(2 * BS * i, 2 * BS)
        ref[rows, :] = jnp.concatenate(planes[2 * i : 2 * i + 2], axis=0).astype(jnp.bfloat16)


def columns_of(plane):
    return [plane[:, 128 * i : 128 * i + 128] for i in range(LANES // 128)]


def tile_ids():
    rows = lax.broadcasted_iota(jnp.int32, (BS, 128), 0)
    lanes = lax.broadcasted_iota(jnp.int32, (BS, 128), 1)
    return rows, lanes


def pack_shell(ref, planes):
    rows, lanes = tile_ids()
    store_pair(ref, pl.ds(0, LANES), planes[0], planes[BS - 1])
    edges, ends = [], []
    for x in range(1, BS - 1):
        columns = columns_of(planes[x])
        edges.append(jnp.where(lanes < C, columns[0], columns[-1]))
        end = columns[0]
        for i, column in enumerate(columns):
            if i:
                end = jnp.where(rows == i, pltpu.roll(column, i, 0), end)
            end = jnp.where(rows == 4 + i, pltpu.roll(column, (i + 5) % BS, 0), end)
        ends.append(end)
    for k in range(3):
        store_pair(ref, pl.ds(LANES + 128 * k, 128), edges[2 * k], edges[2 * k + 1])
        store_pair(ref, pl.ds(LANES + 128 * (3 + k), 128), ends[2 * k], ends[2 * k + 1])


def unpack_shell(ref, packed):
    rows, _ = tile_ids()
    outer = packed[:, pl.ds(0, LANES)].astype(jnp.float32)
    planes = [None] * BS
    planes[0], planes[BS - 1] = outer[:BS], outer[BS:]
    for k in range(3):
        edges = packed[:, pl.ds(LANES + 128 * k, 128)].astype(jnp.float32)
        ends = packed[:, pl.ds(LANES + 128 * (3 + k), 128)].astype(jnp.float32)
        for half in range(2):
            cut = slice(half * BS, half * BS + BS)
            edge, end = edges[cut], ends[cut]
            columns = []
            for i in range(4):
                first = pltpu.roll(end, (BS - i) % BS, 0) if i else end
                last = pltpu.roll(end, (3 - i) % BS, 0) if i != 3 else end
                columns.append(jnp.where(rows == 0, first, jnp.where(rows == BS - 1, last, edge)))
            planes[2 * k + 1 + half] = jnp.concatenate(columns, axis=1)
    store_block(ref, planes)


def upper_first(axis):
    return lax.axis_index(axis) % 2 == 0


def partner_offset(axis, width):
    return jnp.where(upper_first(axis), width, 0)


def outgoing_kernel(lists_ref, words_ref, feat_ref, *refs, axis):
    partner_ref, other_ref, held, shift_ref, lists, words, list_sems, sems = refs[-8:]
    slots = feat_ref.shape[0]
    width = partner_ref.shape[0]
    lists_in = pltpu.make_async_copy(lists_ref, lists, list_sems.at[0])
    words_in = pltpu.make_async_copy(words_ref, words, list_sems.at[1])
    lists_in.start()
    words_in.start()
    lists_in.wait()
    offset = partner_offset(axis, width)
    jobs = []
    for target, start in ((partner_ref, offset), (other_ref, width - offset)):
        for t in range(width):
            name = lists[0, 0, start + t]
            k = len(jobs)
            copy_in = pltpu.make_async_copy(feat_ref.at[jnp.minimum(name, slots - 1)], held.at[k], sems.at[k])
            copy_in.start()
            jobs.append((copy_in, name, target.at[t]))
    for x in range(BS):
        shift_ref[x] = shift_amounts(x)
    words_in.wait()
    for k, (copy_in, name, target) in enumerate(jobs):
        copy_in.wait()

        @pl.when(name < slots)
        def _():
            pack_shell(target, masked_planes(words, name, shift_ref, held.at[k]))


def masked_outgoing(lists, occupancy, features, axis, after=()):
    count = lists.shape[-1]
    half = jax.ShapeDtypeStruct((count // 2,) + SHELL, jnp.bfloat16)
    return pl.pallas_call(
        functools.partial(outgoing_kernel, axis=axis),
        out_shape=(half, half),
        in_specs=[HBM, HBM, HBM] + [ANY] * len(after),
        out_specs=(VMEM, VMEM),
        scratch_shapes=[
            pltpu.VMEM((count, ROWS, LANES), jnp.bfloat16),
            pltpu.VMEM((BS, BS, LANES), jnp.int32),
            pltpu.SMEM(lists.shape, jnp.int32),
            pltpu.SMEM(occupancy.shape, jnp.int32),
            pltpu.SemaphoreType.DMA((2,)),
            pltpu.SemaphoreType.DMA((count,)),
        ],
        compiler_params=pltpu.CompilerParams(vmem_limit_bytes=FIRST_LIMIT),
        cost_estimate=pl.CostEstimate(flops=2000000, bytes_accessed=2 * count * ROWS * LANES * 2, transcendentals=0),
        name="mask_outgoing_" + axis,
    )(lists, occupancy, features, *after)


def unpack_neighbors(pool_ref, start, axis, partner_ref, other_ref):
    width = partner_ref.shape[0]
    offset = partner_offset(axis, width)
    for t in range(width):
        unpack_shell(pool_ref.at[start + offset + t], partner_ref.at[t])
        unpack_shell(pool_ref.at[start + width - offset + t], other_ref.at[t])


def mask_all_kernel(occ_ref, feat_ref, partner_ref, other_ref, earlier_ref, pool_ref, shift_ref):
    slots = feat_ref.shape[0]
    for x in range(BS):
        shift_ref[x] = shift_amounts(x)
    pool_ref[pool_ref.shape[0] - 1] = jnp.zeros((ROWS, LANES), jnp.bfloat16)

    def body(t, carry):
        store_block(pool_ref.at[t], masked_planes(occ_ref, t, shift_ref, feat_ref.at[t]))
        return carry

    lax.fori_loop(0, slots, body, 0)
    unpack_neighbors(pool_ref, slots, "gy", partner_ref, other_ref)


def masked_all(occupancy, features, partner, other, pool_blocks, earlier):
    slots = features.shape[0]
    return pl.pallas_call(
        mask_all_kernel,
        out_shape=jax.ShapeDtypeStruct((pool_blocks, ROWS, LANES), jnp.bfloat16),
        in_specs=[SMEM, VMEM, VMEM, VMEM, ANY],
        out_specs=VMEM,
        scratch_shapes=[pltpu.VMEM((BS, BS, LANES), jnp.int32)],
        compiler_params=params(),
        cost_estimate=pl.CostEstimate(flops=8000000, bytes_accessed=3 * slots * ROWS * LANES * 2, transcendentals=0),
        name="mask_held",
    )(occupancy, features, partner, other, earlier)


def bands_kernel(weights_ref, earlier_ref, out_ref):
    zeros = jnp.zeros((C, C), jnp.float32)
    for pair in range(9):
        taps = [weights_ref[3 * pair + c].astype(jnp.float32) for c in range(3)]
        for z_in in range(GROUP + 2):
            row = [taps[z_in - z_out] if 0 <= z_in - z_out <= 2 else zeros for z_out in range(GROUP)]
            out_ref[pair, pl.ds(z_in * C, C), :] = jnp.concatenate(row, axis=1).astype(jnp.bfloat16)


def banded(weights, earlier):
    return pl.pallas_call(
        bands_kernel,
        out_shape=jax.ShapeDtypeStruct((9, K_BAND, N_BAND), jnp.bfloat16),
        in_specs=[VMEM, ANY],
        out_specs=VMEM,
        compiler_params=params(),
        cost_estimate=pl.CostEstimate(flops=100000, bytes_accessed=4000000, transcendentals=0),
        name="band_weights",
    )(weights, earlier)


def relay_kernel(relays_ref, partner_ref, other_ref, own_partner, own_other, out_partner, out_other, sems, *, slots):
    width = partner_ref.shape[0]
    offset = partner_offset("gx", width)

    def each(act):
        for part, (start, out) in enumerate(((offset, out_partner), (width - offset, out_other))):
            for t in range(width):
                index = relays_ref[0, 0, start + t] - slots
                from_partner = (index >= width) == upper_first("gy")
                place = index % width
                sem = sems.at[part * width + t]

                @pl.when((index >= 0) & from_partner)
                def _():
                    act(pltpu.make_async_copy(partner_ref.at[place], out.at[t], sem))

                @pl.when((index >= 0) & jnp.logical_not(from_partner))
                def _():
                    act(pltpu.make_async_copy(other_ref.at[place], out.at[t], sem))

    each(lambda copy: copy.start())
    each(lambda copy: copy.wait())


def relayed(face_relays, partner, other, own_partner, own_other, slots):
    half = jax.ShapeDtypeStruct(partner.shape, jnp.bfloat16)
    count = face_relays.shape[-1]
    return pl.pallas_call(
        functools.partial(relay_kernel, slots=slots),
        out_shape=(half, half),
        in_specs=[SMEM, ANY, ANY, ANY, ANY],
        out_specs=(ANY, ANY),
        scratch_shapes=[pltpu.SemaphoreType.DMA((count,))],
        input_output_aliases={3: 0, 4: 1},
        compiler_params=params(),
        cost_estimate=pl.CostEstimate(flops=0, bytes_accessed=2 * count * SHELL[0] * SHELL[1] * 2, transcendentals=0),
        name="gather_relays",
    )(face_relays, partner, other, own_partner, own_other)


def extended_plane(blocks, lane_low):
    below, own, above = blocks
    columns = [below] + [own[:, 128 * i : 128 * i + 128] for i in range(4)] + [above]
    turned = [pltpu.roll(column, C, 1) for column in columns]
    return [jnp.where(lane_low, turned[i], turned[i + 1]) for i in range(5)]


def conv_kernel(sent_in, table_in, bias_ref, bands_ref, pool_ref, *refs, jobs, start, waits):
    refs = list(refs)
    sems, table_ref, sent_ref, shift_ref, tiles = (refs.pop() for _ in range(5))
    copies = [
        pltpu.make_async_copy(source, target, sems.at[i])
        for i, (source, target) in enumerate(((sent_in, sent_ref), (table_in, table_ref)))
    ]
    for copy in copies:
        copy.start()
    del refs[:waits]
    if start is None:
        pool = pool_ref
    else:
        pool = refs.pop()
        unpack_neighbors(pool, start, "gx", refs.pop(0), refs.pop(0))
    (out_ref,) = refs
    items = len(jobs)
    pairs = (items + 1) // 2
    for x in range(BS):
        shift_ref[x] = shift_amounts(x)
    for copy in copies:
        copy.wait()
    me = lax.axis_index("gy")
    offsets = table_ref.shape[0] - 27
    slots = [jnp.maximum(sent_ref[item, me ^ distance], 0) for distance, item in jobs]
    slots = slots + slots[-1:] * (2 * pairs - items)

    row_ids = lax.broadcasted_iota(jnp.int32, (BS, 128), 0)
    lane_low = lax.broadcasted_iota(jnp.int32, (2 * BS, 128), 1) < C
    is_last = row_ids == BS - 1
    is_first = row_ids == 0

    def row_pair(slot, depth_x, depth_y, i):
        row = offsets + 9 * depth_x + 3 * depth_y
        rows = pl.ds(2 * BS * i, 2 * BS)
        below = pool[table_ref[row, 0, slot], rows, pl.ds(LANES - 128, 128)]
        own = pool[table_ref[row + 1, 0, slot], rows, :]
        above = pool[table_ref[row + 2, 0, slot], rows, pl.ds(0, 128)]
        return extended_plane([v.astype(jnp.float32) for v in (below, own, above)], lane_low)

    def build(pair, both):
        for depth_x, i in ((0, 3), (1, 0), (1, 1), (1, 2), (1, 3), (2, 0)):
            rows = [[row_pair(slot, depth_x, depth_y, i) for depth_y in range(3)] for slot in both]
            if depth_x == 0:
                planes = ((1, 0),)
            elif depth_x == 2:
                planes = ((0, BS + 1),)
            else:
                planes = ((0, 2 * i + 1), (1, 2 * i + 2))
            for half, plane in planes:
                cut = slice(half * BS, half * BS + BS)
                for column in range(5):
                    lanes = pl.ds(128 * column, 128)
                    shifted = ([], [], [])
                    for k in range(2):
                        before, own, after = (rows[k][depth_y][column][cut] for depth_y in range(3))
                        shifted[0].append(pltpu.roll(jnp.where(is_last, before, own), 1, 0))
                        shifted[1].append(own)
                        shifted[2].append(pltpu.roll(jnp.where(is_first, after, own), BS - 1, 0))
                    for depth_y in range(3):
                        tiles[depth_y, plane, pair, :, lanes] = jnp.concatenate(shifted[depth_y], axis=0).astype(
                            jnp.bfloat16
                        )

    for pair in range(pairs):
        build(pair, slots[2 * pair : 2 * pair + 2])

    bias = bias_ref[...]
    for group in range(BS // GROUP):
        window = pl.ds(group * N_BAND, K_BAND)
        windows = [
            tiles[depth_y, pl.ds(depth_x, BS), :, :, window].reshape(BS * pairs * 2 * BS, K_BAND)
            for depth_x in range(3)
            for depth_y in range(3)
        ]
        total = jnp.dot(
            jnp.concatenate(windows, axis=1),
            bands_ref[...].reshape(9 * K_BAND, N_BAND),
            preferred_element_type=jnp.float32,
        )
        total = (total + bias).reshape(BS, pairs * 2, BS, N_BAND)
        for item in range(items):
            slot = slots[item]
            for i in range(BS // 2):
                parts = []
                for x in (2 * i, 2 * i + 1):
                    bits = plane_bits(table_ref, slot, x, shift_ref[x])[:, group * N_BAND : group * N_BAND + N_BAND]
                    parts.append(jnp.where(bits > 0, total[x, item], 0.0))
                out_ref[item, pl.ds(2 * BS * i, 2 * BS), pl.ds(group * N_BAND, N_BAND)] = jnp.concatenate(
                    parts, axis=0
                ).astype(jnp.bfloat16)


def convolved(jobs, tables, bias, bands, pool, after, shells=(), start=None):
    pairs = (len(jobs) + 1) // 2
    out_shape = [jax.ShapeDtypeStruct((len(jobs), ROWS, LANES), jnp.bfloat16)]
    if shells:
        out_shape.append(jax.ShapeDtypeStruct(pool.shape, pool.dtype))
    return pl.pallas_call(
        functools.partial(conv_kernel, jobs=jobs, start=start, waits=len(after)),
        out_shape=out_shape,
        in_specs=[ANY, ANY, VMEM, VMEM, VMEM] + [ANY] * len(after) + [VMEM] * len(shells),
        out_specs=[VMEM] * len(out_shape),
        scratch_shapes=[
            pltpu.VMEM((3, BS + 2, pairs, 2 * BS, EXT), jnp.bfloat16),
            pltpu.VMEM((BS, BS, LANES), jnp.int32),
            pltpu.SMEM(tables[0].shape, jnp.int32),
            pltpu.SMEM(tables[1].shape, jnp.int32),
            pltpu.SemaphoreType.DMA((2,)),
        ],
        input_output_aliases={4: 1} if shells else {},
        compiler_params=params(),
        cost_estimate=LITTLE,
        name="convolve_%d" % jobs[0][0],
    )(*tables, bias, bands, pool, *after, *shells)


def place_kernel(order_ref, *refs, distances):
    out_ref, sems = refs[-2:]
    names = [order_ref[r] for r in range(out_ref.shape[0])]

    def each(act):
        for distance, source in zip(distances, refs):
            items = source.shape[0]
            first = (lax.axis_index("gy") ^ distance) * items
            for r, name in enumerate(names):

                @pl.when((name >= first) & (name < first + items))
                def _():
                    act(pltpu.make_async_copy(source.at[name - first], out_ref.at[r], sems.at[r]))

    each(lambda copy: copy.start())
    each(lambda copy: copy.wait())


def placed(distances, receive_order, arrived, output):
    count = receive_order.shape[0]
    filled = () if output is None else (output,)
    return pl.pallas_call(
        functools.partial(place_kernel, distances=distances),
        out_shape=jax.ShapeDtypeStruct((count, ROWS, LANES), jnp.bfloat16),
        in_specs=[SMEM] + [ANY] * (len(distances) + len(filled)),
        out_specs=ANY,
        scratch_shapes=[pltpu.SemaphoreType.DMA((count,))],
        input_output_aliases={1 + len(distances): 0} if filled else {},
        compiler_params=params(),
        cost_estimate=LITTLE,
        name="place_%d" % distances[0],
    )(receive_order, *[arrived[m] for m in distances], *filled)


def exchanged(for_partner, for_other, axis):
    count = lax.axis_size(axis)
    others = [(i, i + 1) for i in range(1, count - 1, 2)]
    from_other = lax.ppermute(for_other, axis, others + [(j, i) for i, j in others])
    from_partner = lax.ppermute(for_partner, axis, [(i, i ^ 1) for i in range(count)])
    return from_partner, from_other


def on_device(
    features,
    occupancy,
    neighbors,
    face_lists,
    face_relays,
    send_slots,
    receive_order,
    weights,
    channel_bias,
):
    slots = features.shape[2]
    blocks = features.reshape(slots, ROWS, LANES)
    words = jnp.transpose(occupancy[0], (2, 0, 1))
    peers = send_slots.shape[2]
    faces = face_lists.shape[-1]
    rules = jnp.concatenate([words, jnp.transpose(neighbors[0], (2, 0, 1))], axis=0)
    tables = (jnp.transpose(send_slots[0, 0]), rules)
    bias = jnp.tile(channel_bias, GROUP).reshape(1, N_BAND)

    for_partner, for_other = masked_outgoing(face_lists, words, blocks, "gy")
    own_partner, own_other = masked_outgoing(face_relays, words, blocks, "gx", (for_partner,))
    y_partner, y_other = exchanged(for_partner, for_other, "gy")
    relay_partner, relay_other = relayed(face_relays, y_partner, y_other, own_partner, own_other, slots)
    x_partner, x_other = exchanged(relay_partner, relay_other, "gx")
    pool = masked_all(words, blocks, y_partner, y_other, slots + 2 * faces + 1, relay_partner)
    bands = banded(weights, relay_partner)

    far = list(range(3 * peers // 4, peers)) + list(range(peers // 2, 3 * peers // 4))
    near = list(range(2, peers // 2)) + [1]
    order = far + near + [0]
    arrived, shells, last = {}, (x_partner, x_other), ()
    for i, m in enumerate(order):
        first = i - (len(order) - 2)
        after = last + ((arrived[order[first]],) if 0 <= first < i else ())
        jobs = [(m, item) for item in range(send_slots.shape[3])]
        made = convolved(jobs, tables, bias, bands, pool, after, shells, slots + faces if shells else None)
        last = (made[0],)
        if shells:
            pool, shells = made[1], ()
        arrived[m] = lax.ppermute(made[0], "gy", [(d, d ^ m) for d in range(peers)]) if m else made[0]
    output = placed((0,) + tuple(far[:2]), receive_order[0, 0], arrived, None)
    output = placed(tuple(far[2:-1] + near), receive_order[0, 0], arrived, output)
    output = placed(tuple(far[2:][-1:]), receive_order[0, 0], arrived, output)
    return output.reshape(1, 1, output.shape[0], BS, BS, LANES)


def solution(mesh):
    in_specs = (
        P("gx", "gy", None, None, None, None),
        P("gx", "gy", None, None),
        P("gx", "gy", None, None),
        P("gx", "gy", None),
        P("gx", "gy", None),
        P("gx", "gy", None, None),
        P("gx", "gy", None),
        P(),
        P(),
    )
    out_specs = P("gx", "gy", None, None, None, None)
    return jax.shard_map(
        on_device, mesh=mesh, in_specs=in_specs, out_specs=out_specs, check_vma=False
    )
```

```python
import functools

import jax
import jax.numpy as jnp
from jax import lax
from jax.experimental import pallas as pl
from jax.experimental.pallas import tpu as pltpu
from jax.sharding import PartitionSpec as P

C = 64
BS = 8
ROWS = BS * BS
LANES = BS * C
WORD_BITS = 21
GROUP = 4
K_BAND = (GROUP + 2) * C
N_BAND = GROUP * C
EXT = (BS + 2) * C
SHELL = (2 * BS, LANES + 6 * 128)
VMEM_LIMIT = 16 * 1024 * 1024
FIRST_LIMIT = 56 * 1024 * 1024

LITTLE = pl.CostEstimate(flops=1, bytes_accessed=1, transcendentals=0)

ANY = pl.BlockSpec(memory_space=pl.ANY)
HBM = pl.BlockSpec(memory_space=pltpu.HBM)
SMEM = pl.BlockSpec(memory_space=pltpu.SMEM)
VMEM = pl.BlockSpec(memory_space=pltpu.VMEM)


def params():
    return pltpu.CompilerParams(vmem_limit_bytes=VMEM_LIMIT)


def voxel_ids(x):
    rows = lax.broadcasted_iota(jnp.int32, (BS, LANES), 0)
    lanes = lax.broadcasted_iota(jnp.int32, (BS, LANES), 1)
    return x * ROWS + rows * BS + lanes // C


def shift_amounts(x):
    v = voxel_ids(x)
    first = (x * ROWS) // WORD_BITS
    last = (x * ROWS + ROWS - 1) // WORD_BITS
    amounts = v - first * WORD_BITS
    for k in range(first + 1, last + 1):
        amounts = jnp.where(v >= k * WORD_BITS, v - k * WORD_BITS, amounts)
    return amounts


def plane_bits(occ_ref, slot, x, shifts):
    v = voxel_ids(x)
    first = (x * ROWS) // WORD_BITS
    last = (x * ROWS + ROWS - 1) // WORD_BITS
    words = jnp.full((BS, LANES), occ_ref[first, 0, slot], jnp.int32)
    for k in range(first + 1, last + 1):
        words = jnp.where(v >= k * WORD_BITS, occ_ref[k, 0, slot], words)
    return lax.shift_right_logical(words, shifts) & 1


def masked_planes(occ_ref, slot, shift_ref, source):
    planes = []
    for i in range(BS // 2):
        values = source[pl.ds(2 * BS * i, 2 * BS), :].astype(jnp.float32)
        for half in range(2):
            x = 2 * i + half
            bits = plane_bits(occ_ref, slot, x, shift_ref[x])
            planes.append(jnp.where(bits > 0, values[half * BS : half * BS + BS], 0.0))
    return planes


def store_pair(ref, lanes, first, second):
    ref[:, lanes] = jnp.concatenate([first, second], axis=0).astype(jnp.bfloat16)


def store_block(ref, planes):
    for i in range(BS // 2):
        rows = pl.ds(2 * BS * i, 2 * BS)
        ref[rows, :] = jnp.concatenate(planes[2 * i : 2 * i + 2], axis=0).astype(jnp.bfloat16)


def columns_of(plane):
    return [plane[:, 128 * i : 128 * i + 128] for i in range(LANES // 128)]


def tile_ids():
    rows = lax.broadcasted_iota(jnp.int32, (BS, 128), 0)
    lanes = lax.broadcasted_iota(jnp.int32, (BS, 128), 1)
    return rows, lanes


def pack_shell(ref, planes):
    rows, lanes = tile_ids()
    store_pair(ref, pl.ds(0, LANES), planes[0], planes[BS - 1])
    edges, ends = [], []
    for x in range(1, BS - 1):
        columns = columns_of(planes[x])
        edges.append(jnp.where(lanes < C, columns[0], columns[-1]))
        end = columns[0]
        for i, column in enumerate(columns):
            if i:
                end = jnp.where(rows == i, pltpu.roll(column, i, 0), end)
            end = jnp.where(rows == 4 + i, pltpu.roll(column, (i + 5) % BS, 0), end)
        ends.append(end)
    for k in range(3):
        store_pair(ref, pl.ds(LANES + 128 * k, 128), edges[2 * k], edges[2 * k + 1])
        store_pair(ref, pl.ds(LANES + 128 * (3 + k), 128), ends[2 * k], ends[2 * k + 1])


def unpack_shell(ref, packed):
    rows, _ = tile_ids()
    outer = packed[:, pl.ds(0, LANES)].astype(jnp.float32)
    planes = [None] * BS
    planes[0], planes[BS - 1] = outer[:BS], outer[BS:]
    for k in range(3):
        edges = packed[:, pl.ds(LANES + 128 * k, 128)].astype(jnp.float32)
        ends = packed[:, pl.ds(LANES + 128 * (3 + k), 128)].astype(jnp.float32)
        for half in range(2):
            cut = slice(half * BS, half * BS + BS)
            edge, end = edges[cut], ends[cut]
            columns = []
            for i in range(4):
                first = pltpu.roll(end, (BS - i) % BS, 0) if i else end
                last = pltpu.roll(end, (3 - i) % BS, 0) if i != 3 else end
                columns.append(jnp.where(rows == 0, first, jnp.where(rows == BS - 1, last, edge)))
            planes[2 * k + 1 + half] = jnp.concatenate(columns, axis=1)
    store_block(ref, planes)


def upper_first(axis):
    return lax.axis_index(axis) % 2 == 0


def partner_offset(axis, width):
    return jnp.where(upper_first(axis), width, 0)


def outgoing_kernel(lists_ref, words_ref, feat_ref, *refs, axis):
    partner_ref, other_ref, held, shift_ref, lists, words, list_sems, sems = refs[-8:]
    slots = feat_ref.shape[0]
    width = partner_ref.shape[0]
    lists_in = pltpu.make_async_copy(lists_ref, lists, list_sems.at[0])
    words_in = pltpu.make_async_copy(words_ref, words, list_sems.at[1])
    lists_in.start()
    words_in.start()
    lists_in.wait()
    offset = partner_offset(axis, width)
    jobs = []
    for target, start in ((partner_ref, offset), (other_ref, width - offset)):
        for t in range(width):
            name = lists[0, 0, start + t]
            k = len(jobs)
            copy_in = pltpu.make_async_copy(feat_ref.at[jnp.minimum(name, slots - 1)], held.at[k], sems.at[k])
            copy_in.start()
            jobs.append((copy_in, name, target.at[t]))
    for x in range(BS):
        shift_ref[x] = shift_amounts(x)
    words_in.wait()
    for k, (copy_in, name, target) in enumerate(jobs):
        copy_in.wait()

        @pl.when(name < slots)
        def _():
            pack_shell(target, masked_planes(words, name, shift_ref, held.at[k]))


def masked_outgoing(lists, occupancy, features, axis, after=()):
    count = lists.shape[-1]
    half = jax.ShapeDtypeStruct((count // 2,) + SHELL, jnp.bfloat16)
    return pl.pallas_call(
        functools.partial(outgoing_kernel, axis=axis),
        out_shape=(half, half),
        in_specs=[HBM, HBM, HBM] + [ANY] * len(after),
        out_specs=(VMEM, VMEM),
        scratch_shapes=[
            pltpu.VMEM((count, ROWS, LANES), jnp.bfloat16),
            pltpu.VMEM((BS, BS, LANES), jnp.int32),
            pltpu.SMEM(lists.shape, jnp.int32),
            pltpu.SMEM(occupancy.shape, jnp.int32),
            pltpu.SemaphoreType.DMA((2,)),
            pltpu.SemaphoreType.DMA((count,)),
        ],
        compiler_params=pltpu.CompilerParams(vmem_limit_bytes=FIRST_LIMIT),
        cost_estimate=pl.CostEstimate(flops=2000000, bytes_accessed=2 * count * ROWS * LANES * 2, transcendentals=0),
        name="mask_outgoing_" + axis,
    )(lists, occupancy, features, *after)


def unpack_neighbors(pool_ref, start, axis, partner_ref, other_ref):
    width = partner_ref.shape[0]
    offset = partner_offset(axis, width)
    for t in range(width):
        unpack_shell(pool_ref.at[start + offset + t], partner_ref.at[t])
        unpack_shell(pool_ref.at[start + width - offset + t], other_ref.at[t])


def mask_all_kernel(occ_ref, feat_ref, partner_ref, other_ref, earlier_ref, pool_ref, shift_ref):
    slots = feat_ref.shape[0]
    for x in range(BS):
        shift_ref[x] = shift_amounts(x)
    pool_ref[pool_ref.shape[0] - 1] = jnp.zeros((ROWS, LANES), jnp.bfloat16)

    def body(t, carry):
        store_block(pool_ref.at[t], masked_planes(occ_ref, t, shift_ref, feat_ref.at[t]))
        return carry

    lax.fori_loop(0, slots, body, 0)
    unpack_neighbors(pool_ref, slots, "gy", partner_ref, other_ref)


def masked_all(occupancy, features, partner, other, pool_blocks, earlier):
    slots = features.shape[0]
    return pl.pallas_call(
        mask_all_kernel,
        out_shape=jax.ShapeDtypeStruct((pool_blocks, ROWS, LANES), jnp.bfloat16),
        in_specs=[SMEM, VMEM, VMEM, VMEM, ANY],
        out_specs=VMEM,
        scratch_shapes=[pltpu.VMEM((BS, BS, LANES), jnp.int32)],
        compiler_params=params(),
        cost_estimate=pl.CostEstimate(flops=8000000, bytes_accessed=3 * slots * ROWS * LANES * 2, transcendentals=0),
        name="mask_held",
    )(occupancy, features, partner, other, earlier)


def bands_kernel(weights_ref, earlier_ref, out_ref):
    zeros = jnp.zeros((C, C), jnp.float32)
    for pair in range(9):
        taps = [weights_ref[3 * pair + c].astype(jnp.float32) for c in range(3)]
        for z_in in range(GROUP + 2):
            row = [taps[z_in - z_out] if 0 <= z_in - z_out <= 2 else zeros for z_out in range(GROUP)]
            out_ref[pair, pl.ds(z_in * C, C), :] = jnp.concatenate(row, axis=1).astype(jnp.bfloat16)


def banded(weights, earlier):
    return pl.pallas_call(
        bands_kernel,
        out_shape=jax.ShapeDtypeStruct((9, K_BAND, N_BAND), jnp.bfloat16),
        in_specs=[VMEM, ANY],
        out_specs=VMEM,
        compiler_params=params(),
        cost_estimate=pl.CostEstimate(flops=100000, bytes_accessed=4000000, transcendentals=0),
        name="band_weights",
    )(weights, earlier)


def relay_kernel(relays_ref, partner_ref, other_ref, own_partner, own_other, out_partner, out_other, sems, *, slots):
    width = partner_ref.shape[0]
    offset = partner_offset("gx", width)

    def each(act):
        for part, (start, out) in enumerate(((offset, out_partner), (width - offset, out_other))):
            for t in range(width):
                index = relays_ref[0, 0, start + t] - slots
                from_partner = (index >= width) == upper_first("gy")
                place = index % width
                sem = sems.at[part * width + t]

                @pl.when((index >= 0) & from_partner)
                def _():
                    act(pltpu.make_async_copy(partner_ref.at[place], out.at[t], sem))

                @pl.when((index >= 0) & jnp.logical_not(from_partner))
                def _():
                    act(pltpu.make_async_copy(other_ref.at[place], out.at[t], sem))

    each(lambda copy: copy.start())
    each(lambda copy: copy.wait())


def relayed(face_relays, partner, other, own_partner, own_other, slots):
    half = jax.ShapeDtypeStruct(partner.shape, jnp.bfloat16)
    count = face_relays.shape[-1]
    return pl.pallas_call(
        functools.partial(relay_kernel, slots=slots),
        out_shape=(half, half),
        in_specs=[SMEM, ANY, ANY, ANY, ANY],
        out_specs=(ANY, ANY),
        scratch_shapes=[pltpu.SemaphoreType.DMA((count,))],
        input_output_aliases={3: 0, 4: 1},
        compiler_params=params(),
        cost_estimate=pl.CostEstimate(flops=0, bytes_accessed=2 * count * SHELL[0] * SHELL[1] * 2, transcendentals=0),
        name="gather_relays",
    )(face_relays, partner, other, own_partner, own_other)


def extended_plane(blocks, lane_low):
    below, own, above = blocks
    columns = [below] + [own[:, 128 * i : 128 * i + 128] for i in range(4)] + [above]
    turned = [pltpu.roll(column, C, 1) for column in columns]
    return [jnp.where(lane_low, turned[i], turned[i + 1]) for i in range(5)]


def conv_kernel(sent_in, table_in, bias_ref, bands_ref, pool_ref, *refs, jobs, start, waits):
    refs = list(refs)
    sems, table_ref, sent_ref, shift_ref, tiles = (refs.pop() for _ in range(5))
    copies = [
        pltpu.make_async_copy(source, target, sems.at[i])
        for i, (source, target) in enumerate(((sent_in, sent_ref), (table_in, table_ref)))
    ]
    for copy in copies:
        copy.start()
    del refs[:waits]
    if start is None:
        pool = pool_ref
    else:
        pool = refs.pop()
        unpack_neighbors(pool, start, "gx", refs.pop(0), refs.pop(0))
    (out_ref,) = refs
    items = len(jobs)
    pairs = (items + 1) // 2
    for x in range(BS):
        shift_ref[x] = shift_amounts(x)
    for copy in copies:
        copy.wait()
    me = lax.axis_index("gy")
    offsets = table_ref.shape[0] - 27
    slots = [jnp.maximum(sent_ref[item, me ^ distance], 0) for distance, item in jobs]
    slots = slots + slots[-1:] * (2 * pairs - items)

    row_ids = lax.broadcasted_iota(jnp.int32, (BS, 128), 0)
    lane_low = lax.broadcasted_iota(jnp.int32, (2 * BS, 128), 1) < C
    is_last = row_ids == BS - 1
    is_first = row_ids == 0

    def row_pair(slot, depth_x, depth_y, i):
        row = offsets + 9 * depth_x + 3 * depth_y
        rows = pl.ds(2 * BS * i, 2 * BS)
        below = pool[table_ref[row, 0, slot], rows, pl.ds(LANES - 128, 128)]
        own = pool[table_ref[row + 1, 0, slot], rows, :]
        above = pool[table_ref[row + 2, 0, slot], rows, pl.ds(0, 128)]
        return extended_plane([v.astype(jnp.float32) for v in (below, own, above)], lane_low)

    def build(pair, both):
        for depth_x, i in ((0, 3), (1, 0), (1, 1), (1, 2), (1, 3), (2, 0)):
            rows = [[row_pair(slot, depth_x, depth_y, i) for depth_y in range(3)] for slot in both]
            if depth_x == 0:
                planes = ((1, 0),)
            elif depth_x == 2:
                planes = ((0, BS + 1),)
            else:
                planes = ((0, 2 * i + 1), (1, 2 * i + 2))
            for half, plane in planes:
                cut = slice(half * BS, half * BS + BS)
                for column in range(5):
                    lanes = pl.ds(128 * column, 128)
                    shifted = ([], [], [])
                    for k in range(2):
                        before, own, after = (rows[k][depth_y][column][cut] for depth_y in range(3))
                        shifted[0].append(pltpu.roll(jnp.where(is_last, before, own), 1, 0))
                        shifted[1].append(own)
                        shifted[2].append(pltpu.roll(jnp.where(is_first, after, own), BS - 1, 0))
                    for depth_y in range(3):
                        tiles[depth_y, plane, pair, :, lanes] = jnp.concatenate(shifted[depth_y], axis=0).astype(
                            jnp.bfloat16
                        )

    for pair in range(pairs):
        build(pair, slots[2 * pair : 2 * pair + 2])

    bias = bias_ref[...]
    for group in range(BS // GROUP):
        window = pl.ds(group * N_BAND, K_BAND)
        windows = [
            tiles[depth_y, pl.ds(depth_x, BS), :, :, window].reshape(BS * pairs * 2 * BS, K_BAND)
            for depth_x in range(3)
            for depth_y in range(3)
        ]
        total = jnp.dot(
            jnp.concatenate(windows, axis=1),
            bands_ref[...].reshape(9 * K_BAND, N_BAND),
            preferred_element_type=jnp.float32,
        )
        total = (total + bias).reshape(BS, pairs * 2, BS, N_BAND)
        for item in range(items):
            slot = slots[item]
            for i in range(BS // 2):
                parts = []
                for x in (2 * i, 2 * i + 1):
                    bits = plane_bits(table_ref, slot, x, shift_ref[x])[:, group * N_BAND : group * N_BAND + N_BAND]
                    parts.append(jnp.where(bits > 0, total[x, item], 0.0))
                out_ref[item, pl.ds(2 * BS * i, 2 * BS), pl.ds(group * N_BAND, N_BAND)] = jnp.concatenate(
                    parts, axis=0
                ).astype(jnp.bfloat16)


def convolved(jobs, tables, bias, bands, pool, after, shells=(), start=None):
    pairs = (len(jobs) + 1) // 2
    out_shape = [jax.ShapeDtypeStruct((len(jobs), ROWS, LANES), jnp.bfloat16)]
    if shells:
        out_shape.append(jax.ShapeDtypeStruct(pool.shape, pool.dtype))
    return pl.pallas_call(
        functools.partial(conv_kernel, jobs=jobs, start=start, waits=len(after)),
        out_shape=out_shape,
        in_specs=[ANY, ANY, VMEM, VMEM, VMEM] + [ANY] * len(after) + [VMEM] * len(shells),
        out_specs=[VMEM] * len(out_shape),
        scratch_shapes=[
            pltpu.VMEM((3, BS + 2, pairs, 2 * BS, EXT), jnp.bfloat16),
            pltpu.VMEM((BS, BS, LANES), jnp.int32),
            pltpu.SMEM(tables[0].shape, jnp.int32),
            pltpu.SMEM(tables[1].shape, jnp.int32),
            pltpu.SemaphoreType.DMA((2,)),
        ],
        input_output_aliases={4: 1} if shells else {},
        compiler_params=params(),
        cost_estimate=LITTLE,
        name="convolve_%d" % jobs[0][0],
    )(*tables, bias, bands, pool, *after, *shells)


def place_kernel(order_ref, *refs, distances):
    out_ref, sems = refs[-2:]
    names = [order_ref[r] for r in range(out_ref.shape[0])]

    def each(act):
        for distance, source in zip(distances, refs):
            items = source.shape[0]
            first = (lax.axis_index("gy") ^ distance) * items
            for r, name in enumerate(names):

                @pl.when((name >= first) & (name < first + items))
                def _():
                    act(pltpu.make_async_copy(source.at[name - first], out_ref.at[r], sems.at[r]))

    each(lambda copy: copy.start())
    each(lambda copy: copy.wait())


def placed(distances, receive_order, arrived, output):
    count = receive_order.shape[0]
    filled = () if output is None else (output,)
    return pl.pallas_call(
        functools.partial(place_kernel, distances=distances),
        out_shape=jax.ShapeDtypeStruct((count, ROWS, LANES), jnp.bfloat16),
        in_specs=[SMEM] + [ANY] * (len(distances) + len(filled)),
        out_specs=ANY,
        scratch_shapes=[pltpu.SemaphoreType.DMA((count,))],
        input_output_aliases={1 + len(distances): 0} if filled else {},
        compiler_params=params(),
        cost_estimate=LITTLE,
        name="place_%d" % distances[0],
    )(receive_order, *[arrived[m] for m in distances], *filled)


def exchanged(for_partner, for_other, axis):
    count = lax.axis_size(axis)
    others = [(i, i + 1) for i in range(1, count - 1, 2)]
    from_other = lax.ppermute(for_other, axis, others + [(j, i) for i, j in others])
    from_partner = lax.ppermute(for_partner, axis, [(i, i ^ 1) for i in range(count)])
    return from_partner, from_other


def on_device(
    features,
    occupancy,
    neighbors,
    face_lists,
    face_relays,
    send_slots,
    receive_order,
    weights,
    channel_bias,
):
    slots = features.shape[2]
    blocks = features.reshape(slots, ROWS, LANES)
    words = jnp.transpose(occupancy[0], (2, 0, 1))
    peers = send_slots.shape[2]
    faces = face_lists.shape[-1]
    rules = jnp.concatenate([words, jnp.transpose(neighbors[0], (2, 0, 1))], axis=0)
    tables = (jnp.transpose(send_slots[0, 0]), rules)
    bias = jnp.tile(channel_bias, GROUP).reshape(1, N_BAND)

    for_partner, for_other = masked_outgoing(face_lists, words, blocks, "gy")
    own_partner, own_other = masked_outgoing(face_relays, words, blocks, "gx", (for_partner,))
    y_partner, y_other = exchanged(for_partner, for_other, "gy")
    relay_partner, relay_other = relayed(face_relays, y_partner, y_other, own_partner, own_other, slots)
    x_partner, x_other = exchanged(relay_partner, relay_other, "gx")
    pool = masked_all(words, blocks, y_partner, y_other, slots + 2 * faces + 1, relay_partner)
    bands = banded(weights, relay_partner)

    far = list(range(3 * peers // 4, peers)) + list(range(peers // 2, 3 * peers // 4))
    near = list(range(2, peers // 2)) + [1]
    order = far + near + [0]
    arrived, shells, last = {}, (x_partner, x_other), ()
    for i, m in enumerate(order):
        first = i - (len(order) - 2)
        after = last + ((arrived[order[first]],) if first == 0 < i else ())
        jobs = [(m, item) for item in range(send_slots.shape[3])]
        made = convolved(jobs, tables, bias, bands, pool, after, shells, slots + faces if shells else None)
        last = (made[0],)
        if shells:
            pool, shells = made[1], ()
        arrived[m] = lax.ppermute(made[0], "gy", [(d, d ^ m) for d in range(peers)]) if m else made[0]
    output = placed((0,) + tuple(far[:2]), receive_order[0, 0], arrived, None)
    output = placed(tuple(far[2:-1] + near), receive_order[0, 0], arrived, output)
    output = placed(tuple(far[2:][-1:]), receive_order[0, 0], arrived, output)
    return output.reshape(1, 1, output.shape[0], BS, BS, LANES)


def solution(mesh):
    in_specs = (
        P("gx", "gy", None, None, None, None),
        P("gx", "gy", None, None),
        P("gx", "gy", None, None),
        P("gx", "gy", None),
        P("gx", "gy", None),
        P("gx", "gy", None, None),
        P("gx", "gy", None),
        P(),
        P(),
    )
    out_specs = P("gx", "gy", None, None, None, None)
    return jax.shard_map(
        on_device, mesh=mesh, in_specs=in_specs, out_specs=out_specs, check_vma=False
    )
```
